512 devices in a mesh: rows: 128 (over z, y, core), panels: 4 (over x).
Axes of the slice: x: 4, y: 4, z: 16, core: 2. Of those that a mesh axis runs over, the one named last changes fastest.
Arguments:
- block_column: float32 [131072, 256], P('rows'), may hold values from -4 to 4
- l_panels: float32 [131072, 2, 4, 256], P('rows', None, 'panels'), may hold values from -6 to 6
- u_blocks: float32 [4, 512, 256], P('panels', 'rows'), may hold values from -0.15625 to 0.15625
- diag_inverses: float32 [4, 64, 64], replicated
- leaf_pick: int32 [128, 256], P('rows'), may hold values from 0 to 1023, as said below
- merge_pick: int32 [128, 256], replicated, may hold values from 0 to 511, as said below
- final_order: int32 [256], replicated, may hold values from 0 to 255, each once
Outputs:
- lower_panel: float32 [131072, 256], P(('rows', 'panels'))
- upper_block: float32 [256, 256], replicated
- pivot_rows: int32 [256], replicated
The draws below stay inside these ranges and needn't reach their ends.
Inputs may be any that keep to these rules, and one draw needn't show every extreme that they name: `leaf_pick`: each row holds 256 different row numbers of that block's 1024 rows. `merge_pick`: each row holds 256 different positions among the 512 stacked rows of a merge; row 0 is not read; the picks are given and do not depend on the matrix.
All inputs are finite; a program needn't handle non-finite values.
Results may differ from the reference program's by a relative error of at most 0.0003.
Values sent between devices are 32-bit elements; how exact they have to be, the bound alone decides.
A program may use at most 64 MiB of HBM per device.

```python
import jax
import jax.numpy as jnp
from jax import lax

B = 256
SB = 64
PAN_DEV = 2
ROWS_DEV = 1024
Q = 4
ROWS_ALL = 131072
N_ROWS = 128
N_PANELS = 4


def distinct_rows(key, count, span, keep, special_row):
    keys = jax.random.split(key, count)
    drawn = jax.vmap(lambda row_key: jax.random.permutation(row_key, span)[:keep])(keys).astype(jnp.int32)
    inner = (jax.random.permutation(jax.random.fold_in(key, 7), span - 2)[:keep - 2] + 1).astype(jnp.int32)
    ends = jnp.array([0, span - 1], dtype=jnp.int32)
    special = jax.random.permutation(jax.random.fold_in(key, 9), jnp.concatenate([inner, ends])).astype(jnp.int32)
    row_numbers = jnp.arange(count, dtype=jnp.int32)[:, None]
    return jnp.where(row_numbers == special_row, special[None, :], drawn).astype(jnp.int32)


def draw_leaf_pick(key, part):
    key = jax.random.fold_in(key, 11)
    return distinct_rows(key, N_ROWS, ROWS_DEV, B, 0)


def draw_merge_pick(key, part):
    key = jax.random.fold_in(key, 17)
    return distinct_rows(key, N_ROWS, 2 * B, B, 1)


def draw_diag_inverses(key, part):
    key = jax.random.fold_in(key, 23)
    first_key, second_key = jax.random.split(key)
    diagonal = jnp.exp(jax.random.uniform(first_key, (Q, SB, 1), jnp.float32, jnp.log(0.5), jnp.log(1.0)))
    beside = jax.random.normal(second_key, (Q, SB, SB), jnp.float32) * (0.3 / SB ** 0.5)
    identity = jnp.eye(SB, dtype=jnp.float32)[None]
    return ((diagonal * identity + beside * (1.0 - identity)) / SB ** 0.5).astype(jnp.float32)


def level_of(own_key, extent, shards, least, largest):
    level, own = 1.0, jax.random.fold_in(own_key, 6)
    for axis_at, blocks in shards:
        steps = jnp.exp(jax.random.uniform(jax.random.fold_in(own, axis_at), (blocks,), jnp.float32, least / len(shards), largest / len(shards)))
        level = level * jnp.repeat(steps, extent[axis_at] // blocks).reshape([-1 if axis == axis_at else 1 for axis in range(len(extent))])
    return level


def centred(own_key, dims, deviation, reach, cuts=(), held_as=jnp.bfloat16):
    drawn = deviation * jax.random.normal(own_key, dims, jnp.float32)
    if cuts:
        drawn = drawn * level_of(own_key, dims, cuts, -0.22, 0.18)
    return jnp.clip(drawn, -reach, reach).astype(held_as)


def setup_inputs(seed: int = 0) -> dict:
    key_list = jax.random.split(jax.random.key(seed), 8)
    return {
        "block_column": centred(key_list[0], (ROWS_ALL, B), 0.5, 4.0, ((0, 128),), jnp.float32),
        "l_panels": centred(key_list[1], (ROWS_ALL, PAN_DEV, N_PANELS, B), 1.0, 6.0, ((0, 128), (2, 4)), jnp.float32),
        "u_blocks": centred(key_list[2], (N_PANELS, PAN_DEV * B, B), (0.5 / (PAN_DEV * N_PANELS * B) ** 0.5), 0.15625, ((0, 4), (1, 128)), jnp.float32),
        "diag_inverses": draw_diag_inverses(jax.random.fold_in(key_list[7], 71), 0),
        "leaf_pick": draw_leaf_pick(jax.random.fold_in(key_list[7], 71), 0),
        "merge_pick": draw_merge_pick(jax.random.fold_in(key_list[7], 71), 0),
        "final_order": jax.random.permutation(key_list[6], B).astype(jnp.int32),
    }


def make_uppers(winners, inverses):
    sub = inverses.shape[1]
    panel_width = winners.shape[1]
    columns = jnp.arange(panel_width, dtype=jnp.int32)
    remaining = winners
    uppers = []
    for section in range(inverses.shape[0]):
        lower_part = jnp.dot(remaining[:, section * sub:(section + 1) * sub], inverses[section], precision=lax.Precision.HIGHEST, preferred_element_type=jnp.float32)
        keep_mask = (columns >= section * sub).astype(jnp.float32)
        uppers.append(remaining[section * sub:(section + 1) * sub] * keep_mask[None, :])
        later = (columns >= (section + 1) * sub).astype(jnp.float32)
        remaining = remaining - jnp.dot(lower_part, uppers[-1] * later[None, :], precision=lax.Precision.HIGHEST, preferred_element_type=jnp.float32)
    return uppers


def sweep_rows(remaining, inverses, uppers):
    sub = inverses.shape[1]
    columns = jnp.arange(remaining.shape[1], dtype=jnp.int32)
    lowers = []
    for section in range(inverses.shape[0]):
        lower_part = jnp.dot(remaining[:, section * sub:(section + 1) * sub], inverses[section], precision=lax.Precision.HIGHEST, preferred_element_type=jnp.float32)
        lowers.append(lower_part)
        later = (columns >= (section + 1) * sub).astype(jnp.float32)
        remaining = remaining - jnp.dot(lower_part, uppers[section] * later[None, :], precision=lax.Precision.HIGHEST, preferred_element_type=jnp.float32)
    return jnp.concatenate(lowers, axis=1)


def reference(block_column, l_panels, u_blocks, diag_inverses, leaf_pick, merge_pick, final_order):
    all_rows = N_ROWS * ROWS_DEV
    l_matrix = l_panels.reshape(all_rows, PAN_DEV * N_PANELS * B)
    u_matrix = u_blocks.reshape(N_PANELS, PAN_DEV, B, B).transpose(1, 0, 2, 3).reshape(PAN_DEV * N_PANELS * B, B)
    updated = block_column - jnp.dot(l_matrix, u_matrix, precision=lax.Precision.HIGHEST, preferred_element_type=jnp.float32)
    blocks = updated.reshape(N_ROWS, ROWS_DEV, B)
    candidates = jnp.take_along_axis(blocks, leaf_pick[:, :, None], axis=1)
    anchor = leaf_pick + (jnp.arange(N_ROWS, dtype=jnp.int32) * ROWS_DEV)[:, None]
    for depth in range(N_ROWS.bit_length() - 1):
        stride = 2 ** depth
        merged = jnp.concatenate([candidates[0::2], candidates[1::2]], axis=1)
        merged_anchor = jnp.concatenate([anchor[0::2], anchor[1::2]], axis=1)
        owners = jnp.arange(candidates.shape[0] // 2, dtype=jnp.int32) * (2 * stride) + stride
        chosen = merge_pick[owners]
        candidates = jnp.take_along_axis(merged, chosen[:, :, None], axis=1)
        anchor = jnp.take_along_axis(merged_anchor, chosen, axis=1)
    pivot_block = candidates[0][final_order]
    pivot_rows = anchor[0][final_order].astype(jnp.int32)
    uppers = make_uppers(pivot_block, diag_inverses)
    lower_panel = sweep_rows(updated, diag_inverses, uppers)
    upper_block = jnp.concatenate(uppers, axis=0)
    return lower_panel, upper_block, pivot_rows
```

```python
import functools

import jax
import jax.numpy as jnp
from jax import lax
from jax.experimental import pallas as pl
from jax.experimental.pallas import tpu as pltpu
from jax.sharding import PartitionSpec as P

MESH = pl.DeviceIdType.MESH
F32, BF16, I32 = jnp.float32, jnp.bfloat16, jnp.int32
NZ, NY, NC, NX = 16, 4, 2, 4
FAR_FIRST = (8, 7, 9, 6, 10, 5, 11, 4, 12, 3, 13, 2, 14, 1, 15)


def halves(v):
    hi = v.astype(BF16)
    return hi, (v - hi.astype(F32)).astype(BF16)


def mm(a, b):
    return jnp.dot(a, b, preferred_element_type=F32)


def mm3(a, b):
    ah, al = halves(a)
    bh, bl = halves(b)
    return mm(ah, bh) + (mm(al, bh) + mm(ah, bl))


def kernel(
    l_hbm, bc_hbm, u_hbm, d_hbm, leaf_hbm, mp_hbm, fo_hbm,
    low_ref, up_ref, piv_ref,
    l_raw, aux_raw, own, dinv, leaf, mp, fo, u_raw,
    xhi, xlo, g, lp, lpm, pay, rc, b1, ry, b2, sz, rz, uhi, ulo, prod, xr, xb, w, xs,
    in_sem, uz_s, uz_r, uy_s, uy_r, uc_s, uc_r, lz_s, lz_r, ly_s, ly_r, lc_s, lc_r,
    pc_s, pc_r, py_s, py_r, pz_s, pz_r, x_s, x_r, wz_s, wz_r, wy_s, wy_r, wc_s, wc_r, rx_s, rx_r,
):
    row = lax.axis_index("rows")
    x = lax.axis_index("panels")
    z, y, c = row // (NY * NC), (row // NC) % NY, row % NC
    rows_dev = bc_hbm.shape[0]
    quarter = rows_dev // NX

    def dev(zz, yy, cc, xx):
        return ((zz * NY + yy) * NC + cc, xx)

    def zp(k):
        return (z + k) % NZ

    def yp(k):
        return (y + k) % NY

    def xp(k):
        return (x + k) % NX

    to_z = [dev(zp(k), y, c, x) for k in range(NZ)]
    to_y = [dev(z, yp(k), c, x) for k in range(NY)]
    to_x = [dev(z, y, c, xp(k)) for k in range(NX)]
    to_c = dev(z, y, 1 - c, x)

    col = pl.multiple_of((x % 2) * 128, 128)
    mine = pl.multiple_of(x * quarter, quarter)
    loads = [
        pltpu.make_async_copy(mp_hbm, mp, in_sem.at[0]),
        pltpu.make_async_copy(fo_hbm, fo, in_sem.at[1]),
        pltpu.make_async_copy(leaf_hbm, leaf, in_sem.at[2]),
        pltpu.make_async_copy(u_hbm, u_raw, in_sem.at[3]),
        pltpu.make_async_copy(l_hbm, l_raw, in_sem.at[4]),
        pltpu.make_async_copy(bc_hbm.at[:, pl.ds(col, 128)], aux_raw, in_sem.at[5]),
        pltpu.make_async_copy(bc_hbm.at[pl.ds(mine, quarter), :], own, in_sem.at[6]),
        pltpu.make_async_copy(d_hbm, dinv, in_sem.at[7]),
    ]
    for copy in loads:
        copy.start()

    barrier = pltpu.get_barrier_semaphore()
    partners = [to_z[k] for k in FAR_FIRST] + to_y[1:] + to_x[1:] + [to_c]
    for partner in partners:
        pl.semaphore_signal(barrier, inc=1, device_id=partner, device_id_type=MESH)

    def remote(src, dst, send, recv, to):
        return pltpu.make_async_remote_copy(src, dst, send, recv, device_id=to, device_id_type=MESH)

    sub = lax.broadcasted_iota(I32, (256, 256), 0).astype(F32)
    for copy in loads[:4]:
        copy.wait()
    table = mp[...]
    table = jnp.concatenate([(table >> 8).astype(F32), (table & 255).astype(F32)], axis=0).astype(BF16)
    block = jnp.zeros((1, 256), F32)
    pos = fo[...].astype(F32)

    def pick(at):
        return jnp.where(sub == at, 1.0, 0.0).astype(BF16)

    def looked_up(table, at, owner):
        found = mm(table, pick(at))
        found = 256.0 * found[:128] + found[128:]
        return jnp.sum(jnp.where(sub[:128] == owner, found, 0.0), axis=0, keepdims=True)

    for level in reversed(range(7)):
        owner = block * (2.0 ** (level + 1)) + 2.0**level
        found = looked_up(table, pos, owner)
        upper = jnp.where(found >= 256.0, 1.0, 0.0)
        block = 2.0 * block + upper
        pos = found - 256.0 * upper
    chosen = pick(pos)
    own_leaf = jnp.broadcast_to(leaf[...], (16, 256))
    own_leaf = jnp.where(sub[:16].astype(I32) == 0, own_leaf >> 8, own_leaf & 255).astype(F32).astype(BF16)
    own_row = mm(own_leaf, chosen)
    own_row = 256.0 * own_row[0:1] + own_row[1:2]
    own_row = jnp.where(block == row.astype(F32), own_row, -1.0)
    row_col = jnp.broadcast_to(own_row, (128, 256)).T

    for i in range(4):
        for h in range(2):
            g[z, y, c, 2 * i + h : 2 * i + h + 1, :] = u_raw[i : i + 1, 128 * h : 128 * h + 128]
    lp[z, y, c] = leaf[...]
    pl.semaphore_wait(barrier, len(partners))
    sends = []

    def go(copy):
        copy.start()
        sends.append(copy)

    for k in FAR_FIRST:
        go(remote(g.at[z, y, c], g.at[z, y, c], uz_s.at[k], uz_r.at[k], to_z[k]))

    for copy in loads[4:]:
        copy.wait()

    @pl.loop(0, NX)
    def _(part):
        rows = pl.ds(pl.multiple_of(part * quarter, quarter), quarter)
        for j in range(4):
            hi, lo = halves(l_raw[pl.ds(part * quarter * 4 + j, quarter, stride=4), :])
            xhi[rows, 128 * j : 128 * j + 128] = hi
            xlo[rows, 128 * j : 128 * j + 128] = lo
        hi, lo = halves(jnp.where(x < 2, aux_raw[rows, :], 0.0))
        xhi[rows, 512:640] = hi
        xlo[rows, 512:640] = lo

    lane = lax.broadcasted_iota(I32, (256, 128), 1).astype(F32)
    select = jnp.concatenate(
        [jnp.where(row_col == lane + 128.0 * j, 1.0, 0.0).astype(BF16) for j in range(rows_dev // 128)], axis=1
    )
    pay[...] = mm(select, xhi[...]) + mm(select, xlo[...])
    there = pl.ds(pl.multiple_of((1 - c) * 128, 128), 128)
    here = pl.ds(pl.multiple_of(c * 128, 128), 128)
    pc = remote(pay.at[there, :], rc, pc_s.at[0], pc_r.at[0], to_c)
    go(pc)
    for k in FAR_FIRST:
        go(remote(lp.at[z, y, c], lp.at[z, y, c], lz_s.at[k], lz_r.at[k], to_z[k]))
    pc.wait_recv()
    b1[...] = pay[here, :] + rc[...]
    py = []
    for k in (2, 1, 3):
        src = b1.at[pl.ds(pl.multiple_of(yp(k) * 32, 32), 32), :]
        py.append(remote(src, ry.at[k], py_s.at[k], py_r.at[k], to_y[k]))
        go(py[-1])

    for k in FAR_FIRST[::-1]:
        slot = g.at[zp(NZ - k), y, c]
        remote(slot, slot, uz_s.at[k], uz_r.at[k], to_z[k]).wait_recv()
    for k in (2, 1, 3):
        go(remote(g.at[:, y, c], g.at[:, y, c], uy_s.at[k], uy_r.at[k], to_y[k]))

    for copy in py:
        copy.wait_recv()
    b2[...] = b1[pl.ds(pl.multiple_of(y * 32, 32), 32), :] + ry[1] + ry[2] + ry[3]
    for zz in range(NZ):
        for j in range(5):
            sz[zz, j] = b2[2 * zz : 2 * zz + 2, 128 * j : 128 * j + 128]
    pz = []
    for k in FAR_FIRST:
        pz.append(remote(sz.at[zp(k)], rz.at[k], pz_s.at[k], pz_r.at[k], to_z[k]))
        go(pz[-1])

    for k in (1, 3, 2):
        slot = g.at[:, yp(NY - k), c]
        remote(slot, slot, uy_s.at[k], uy_r.at[k], to_y[k]).wait_recv()
    go(remote(g.at[:, :, c], g.at[:, :, c], uc_s.at[0], uc_r.at[0], to_c))

    for k in FAR_FIRST[::-1]:
        slot = lp.at[zp(NZ - k), y, c]
        remote(slot, slot, lz_s.at[k], lz_r.at[k], to_z[k]).wait_recv()
    for k in (2, 1, 3):
        go(remote(lp.at[:, y, c], lp.at[:, y, c], ly_s.at[k], ly_r.at[k], to_y[k]))

    slot = g.at[:, :, 1 - c]
    remote(slot, slot, uc_s.at[0], uc_r.at[0], to_c).wait_recv()
    flat = g.reshape(NZ * NY * NC * 8, 128)
    for h in range(2):
        hi, lo = halves(flat[pl.ds(h, 512, stride=2), :])
        uhi[:, 128 * h : 128 * h + 128] = hi
        ulo[:, 128 * h : 128 * h + 128] = lo

    @pl.loop(0, NX)
    def _(part):
        rows = pl.ds(pl.multiple_of(part * quarter, quarter), quarter)
        left, right = xhi[rows, :512], uhi[...]
        prod[rows, :] = mm(left, right) + (mm(xlo[rows, :512], right) + mm(left, ulo[...]))

    mine2 = sz[z]
    for copy in pz:
        copy.wait_recv()
    for k in range(1, NZ):
        mine2 = mine2 + rz[k]
    two = jnp.concatenate([mine2[j] for j in range(4)], axis=1)
    two_hi = two.astype(BF16).astype(F32)
    stacked = jnp.concatenate([two_hi, two - two_hi, jnp.zeros((12, 512), F32)], axis=0).astype(BF16)
    by_hi = mm(stacked, uhi[...])
    by_lo = mm(stacked, ulo[...])
    two = by_hi[0:2] + (by_hi[2:4] + by_lo[0:2])
    for h in range(2):
        xb[x, 2 * h : 2 * h + 2, :] = jnp.where(x == h, mine2[4], 0.0) - two[:, 128 * h : 128 * h + 128]
    px = []
    for k in (2, 1, 3):
        px.append(remote(xb.at[x], xb.at[x], x_s.at[k], x_r.at[k], to_x[k]))
        go(px[-1])
    for k in (1, 3, 2):
        slot = xb.at[xp(NX - k)]
        remote(slot, slot, x_s.at[k], x_r.at[k], to_x[k]).wait_recv()
    w[c, y, z] = xb[0] + xb[1] + xb[2] + xb[3]
    for k in FAR_FIRST:
        go(remote(w.at[c, y, z], w.at[c, y, z], wz_s.at[k], wz_r.at[k], to_z[k]))
    rx = []
    for k in (2, 1, 3):
        src = prod.at[pl.ds(pl.multiple_of(xp(k) * quarter, quarter), quarter), :]
        rx.append(remote(src, xr.at[k], rx_s.at[k], rx_r.at[k], to_x[k]))
        go(rx[-1])

    for k in (1, 3, 2):
        slot = lp.at[:, yp(NY - k), c]
        remote(slot, slot, ly_s.at[k], ly_r.at[k], to_y[k]).wait_recv()
    go(remote(lp.at[:, :, c], lp.at[:, :, c], lc_s.at[0], lc_r.at[0], to_c))
    slot = lp.at[:, :, 1 - c]
    remote(slot, slot, lc_s.at[0], lc_r.at[0], to_c).wait_recv()

    for slot in range(NZ * NY * NC):
        lpm[slot : slot + 1, :] = lp[slot // (NY * NC), slot // NC % NY, slot % NC]

    leaves = lpm[...]
    leaves = jnp.concatenate([(leaves >> 8).astype(F32), (leaves & 255).astype(F32)], axis=0).astype(BF16)
    number = float(rows_dev) * block + looked_up(leaves, pos, block)
    piv_ref[...] = number.astype(I32)

    for k in FAR_FIRST[::-1]:
        slot = w.at[c, y, zp(NZ - k)]
        remote(slot, slot, wz_s.at[k], wz_r.at[k], to_z[k]).wait_recv()
    for k in (2, 1, 3):
        go(remote(w.at[c, y], w.at[c, y], wy_s.at[k], wy_r.at[k], to_y[k]))
    for k in (1, 3, 2):
        slot = w.at[c, yp(NY - k)]
        remote(slot, slot, wy_s.at[k], wy_r.at[k], to_y[k]).wait_recv()
    go(remote(w.at[c], w.at[c], wc_s.at[0], wc_r.at[0], to_c))

    for copy in rx:
        copy.wait_recv()
    xs[pl.ds(256, quarter), :] = own[...] - (prod[pl.ds(mine, quarter), :] + xr[1] + xr[2] + xr[3])

    slot = w.at[1 - c]
    remote(slot, slot, wc_s.at[0], wc_r.at[0], to_c).wait_recv()

    for slot in range(NC * NY * NZ):
        for h in range(2):
            piece = w[slot // (NY * NZ), slot // NZ % NY, slot % NZ, 2 * h : 2 * h + 2, :]
            xs[2 * slot : 2 * slot + 2, 128 * h : 128 * h + 128] = piece

    column = lax.broadcasted_iota(I32, (64, 256), 1)
    rest = xs[...]
    for t in range(4):
        inverse = dinv[t]
        panel = rest[:, 64 * t : 64 * t + 64]
        u_t = rest[64 * t : 64 * t + 64, :]
        up_ref[64 * t : 64 * t + 64, :] = jnp.where(column >= 64 * t, u_t, 0.0)
        low_ref[:, 64 * t : 64 * t + 64] = mm3(panel[256:], inverse)
        if t < 3:
            step = mm3(inverse, jnp.where(column >= 64 * (t + 1), u_t, 0.0))
            rest = rest - mm3(panel, step)

    for copy in sends:
        copy.wait_send()


def body(block_column, l_panels, u_blocks, diag_inverses, leaf_pick, merge_pick, final_order):
    rows_dev, cols = block_column.shape
    quarter = rows_dev // NX
    vmem = pl.BlockSpec(memory_space=pltpu.VMEM)
    sem = pltpu.SemaphoreType.DMA
    low, up, piv = pl.pallas_call(
        kernel,
        name="panel",
        out_shape=(
            jax.ShapeDtypeStruct((quarter, cols), F32),
            jax.ShapeDtypeStruct((cols, cols), F32),
            jax.ShapeDtypeStruct((1, cols), I32),
        ),
        in_specs=[pl.BlockSpec(memory_space=pl.ANY)] * 7,
        out_specs=(vmem, vmem, vmem),
        scratch_shapes=[
            pltpu.VMEM((rows_dev * 4, 128), F32),
            pltpu.VMEM((rows_dev, 128), F32),
            pltpu.VMEM((quarter, cols), F32),
            pltpu.VMEM(diag_inverses.shape, F32),
            pltpu.VMEM((1, 256), I32),
            pltpu.VMEM((128, 256), I32),
            pltpu.VMEM((1, 256), I32),
            pltpu.VMEM((4, 256), F32),
            pltpu.VMEM((rows_dev, 640), BF16),
            pltpu.VMEM((rows_dev, 640), BF16),
            pltpu.VMEM((NZ, NY, NC, 8, 128), F32),
            pltpu.VMEM((NZ, NY, NC, 1, 256), I32),
            pltpu.VMEM((128, 256), I32),
            pltpu.VMEM((256, 640), F32),
            pltpu.VMEM((128, 640), F32),
            pltpu.VMEM((128, 640), F32),
            pltpu.VMEM((NY, 32, 640), F32),
            pltpu.VMEM((32, 640), F32),
            pltpu.VMEM((NZ, 5, 2, 128), F32),
            pltpu.VMEM((NZ, 5, 2, 128), F32),
            pltpu.VMEM((512, cols), BF16),
            pltpu.VMEM((512, cols), BF16),
            pltpu.VMEM((rows_dev, cols), F32),
            pltpu.VMEM((NX, quarter, cols), F32),
            pltpu.VMEM((NX, 4, 128), F32),
            pltpu.VMEM((NC, NY, NZ, 4, 128), F32),
            pltpu.VMEM((256 + quarter, cols), F32),
            sem((8,)),
            sem((NZ,)), sem((NZ,)), sem((NY,)), sem((NY,)), sem((1,)), sem((1,)),
            sem((NZ,)), sem((NZ,)), sem((NY,)), sem((NY,)), sem((1,)), sem((1,)),
            sem((1,)), sem((1,)), sem((NY,)), sem((NY,)), sem((NZ,)), sem((NZ,)),
            sem((NX,)), sem((NX,)),
            sem((NZ,)), sem((NZ,)), sem((NY,)), sem((NY,)), sem((1,)), sem((1,)),
            sem((NX,)), sem((NX,)),
        ],
        compiler_params=pltpu.CompilerParams(
            collective_id=0, has_side_effects=True, vmem_limit_bytes=56 * 1024 * 1024
        ),
    )(
        block_column_rows(l_panels),
        block_column,
        u_blocks[0],
        diag_inverses,
        leaf_pick,
        merge_pick,
        final_order.reshape(1, -1),
    )
    return low, up, piv[0]


def block_column_rows(l_panels):
    return l_panels.reshape(-1, 128)


def solution(mesh):
    return jax.shard_map(
        body,
        mesh=mesh,
        in_specs=(
            P("rows", None),
            P("rows", None, "panels", None),
            P("panels", "rows", None),
            P(),
            P("rows", None),
            P(),
            P(),
        ),
        out_specs=(P(("rows", "panels"), None), P(), P()),
        check_vma=False,
    )
```

```python
import functools

import jax
import jax.numpy as jnp
from jax import lax
from jax.experimental import pallas as pl
from jax.experimental.pallas import tpu as pltpu
from jax.sharding import PartitionSpec as P

MESH = pl.DeviceIdType.MESH
F32, BF16, I32 = jnp.float32, jnp.bfloat16, jnp.int32
NZ, NY, NC, NX = 16, 4, 2, 4
FAR_FIRST = (8, 7, 9, 6, 10, 5, 11, 4, 12, 3, 13, 2, 14, 1, 15)
NEAR = (4, 12, 3, 13, 2, 14, 1, 15)
RANGES = {"low": (0, 5), "high": (12, 16), "up": (5, 9), "down": (9, 12)}


def halves(v):
    hi = v.astype(BF16)
    return hi, (v - hi.astype(F32)).astype(BF16)


def mm(a, b):
    return jnp.dot(a, b, preferred_element_type=F32)


def mm3(a, b):
    ah, al = halves(a)
    bh, bl = halves(b)
    return mm(ah, bh) + (mm(al, bh) + mm(ah, bl))


def kernel(
    l_hbm, bc_hbm, u_hbm, leaf_hbm, mp_hbm, fo_hbm,
    xs, piv_ref,
    l_raw, aux_raw, own, leaf, mp, fo, u_raw,
    xhi, xlo, g, lp, lpm, pay, rc, b1, ry, b2, sz, rz, uhi, ulo, prod, xr, xb, w,
    in_sem, uz_s, uz_r, ub_s, ub_r, uy_s, uy_r, uc_s, uc_r, lz_s, lz_r, ly_s, ly_r, lc_s, lc_r,
    pc_s, pc_r, py_s, py_r, pz_s, pz_r, x_s, x_r, wz_s, wz_r, wy_s, wy_r, wc_s, wc_r, rx_s, rx_r,
):
    row = lax.axis_index("rows")
    x = lax.axis_index("panels")
    z, y, c = row // (NY * NC), (row // NC) % NY, row % NC
    rows_dev = bc_hbm.shape[0]
    quarter = rows_dev // NX

    def dev(zz, yy, cc, xx):
        return ((zz * NY + yy) * NC + cc, xx)

    def zp(k):
        return (z + k) % NZ

    def yp(k):
        return (y + k) % NY

    def xp(k):
        return (x + k) % NX

    to_z = [dev(zp(k), y, c, x) for k in range(NZ)]
    to_y = [dev(z, yp(k), c, x) for k in range(NY)]
    to_x = [dev(z, y, c, xp(k)) for k in range(NX)]
    to_c = dev(z, y, 1 - c, x)

    col = pl.multiple_of((x % 2) * 128, 128)
    mine = pl.multiple_of(x * quarter, quarter)
    loads = [
        pltpu.make_async_copy(mp_hbm.at[:, pl.ds(0, 128)], mp.at[0], in_sem.at[0]),
        pltpu.make_async_copy(fo_hbm, fo, in_sem.at[1]),
        pltpu.make_async_copy(leaf_hbm, leaf, in_sem.at[2]),
        pltpu.make_async_copy(u_hbm, u_raw, in_sem.at[3]),
        pltpu.make_async_copy(mp_hbm.at[:, pl.ds(128, 128)], mp.at[1], in_sem.at[7]),
        pltpu.make_async_copy(l_hbm, l_raw, in_sem.at[4]),
        pltpu.make_async_copy(bc_hbm.at[:, pl.ds(col, 128)], aux_raw, in_sem.at[5]),
        pltpu.make_async_copy(bc_hbm.at[pl.ds(mine, quarter), :], own, in_sem.at[6]),
    ]
    for copy in loads:
        copy.start()

    barrier = pltpu.get_barrier_semaphore()
    partners = [to_z[k] for k in NEAR] + to_y[1:] + to_x[1:] + [to_c]
    for partner in partners:
        pl.semaphore_signal(barrier, inc=1, device_id=partner, device_id_type=MESH)

    sends = []
    arrivals = {}

    def send(name, src, dst, send_sem, recv_sem, to, lands):
        copy = pltpu.make_async_remote_copy(src, dst, send_sem, recv_sem, device_id=to, device_id_type=MESH)
        copy.start()
        sends.append(copy)
        came = pltpu.make_async_remote_copy(lands, lands, send_sem, recv_sem, device_id=to, device_id_type=MESH)
        arrivals.setdefault(name, []).append(came)

    def arrive(*names):
        for name in names:
            for copy in arrivals.pop(name)[::-1]:
                copy.wait_recv()

    for copy in loads[3:4]:
        copy.wait()
    for i in range(4):
        for h in range(2):
            g[0, y, c, 2 * i + h : 2 * i + h + 1, :] = u_raw[i : i + 1, 128 * h : 128 * h + 128]

    for copy in loads[:3] + loads[4:5]:
        copy.wait()
    lp[0, y, c] = leaf[...]
    down = lax.broadcasted_iota(I32, (8, 128), 0)

    def picked(half0, half1, at):
        low = at & 127
        return jnp.where(at >= 128, jnp.take_along_axis(half1, low, axis=1), jnp.take_along_axis(half0, low, axis=1))

    def looked_up(table, first, stride, count, owner, at):
        if count < 8:
            total = jnp.zeros((8, 128), F32)
            for i in range(count):
                line = first + i * stride
                rows = [jnp.broadcast_to(table[h, line : line + 1, :], (8, 128)) for h in range(2)]
                total = jnp.where(owner == i, picked(*rows, at).astype(F32), total)
            return total
        total = jnp.zeros((8, 128), F32)
        for i in range(0, count, 8):
            rows = [table[h, pl.ds(first + i * stride, 8, stride=stride), :] for h in range(2)]
            total += jnp.where(owner - i == down, picked(*rows, at).astype(F32), 0.0)
        return jnp.broadcast_to(jnp.sum(total, axis=0, keepdims=True), (8, 128))

    blocks, places, own_rows = [], [], []
    for s in range(2):
        at = jnp.broadcast_to(fo[:, 128 * s : 128 * s + 128], (8, 128))
        block = jnp.zeros((8, 128), I32)
        for level in reversed(range(7)):
            found = looked_up(mp, 1 << level, 2 << level, 64 >> level, block, at).astype(I32)
            block = 2 * block + (found >> 8)
            at = found & 255
        rows = [jnp.broadcast_to(leaf[:, 128 * h : 128 * h + 128], (8, 128)) for h in range(2)]
        blocks.append(block)
        places.append(at)
        own_rows.append(jnp.where(block == row, picked(*rows, at), -1))
    own_row = jnp.concatenate([v[0:1] for v in own_rows], axis=1).astype(F32)
    row_col = jnp.broadcast_to(own_row, (128, 256)).T

    pl.semaphore_wait(barrier, len(partners))
    for k in NEAR:
        at = NZ - k
        send(("uz", at), g.at[0, y, c], g.at[at, y, c], uz_s.at[k], uz_r.at[k], to_z[k], g.at[at, y, c])

    for copy in loads[5:]:
        copy.wait()

    for part in range(NX):
        rows = pl.ds(part * quarter, quarter)
        for j in range(4):
            hi, lo = halves(l_raw[pl.ds(part * quarter * 4 + j, quarter, stride=4), :])
            xhi[rows, 128 * j : 128 * j + 128] = hi
            xlo[rows, 128 * j : 128 * j + 128] = lo
        hi, lo = halves(jnp.where(x < 2, aux_raw[rows, :], 0.0))
        xhi[rows, 512:640] = hi
        xlo[rows, 512:640] = lo

    lane = lax.broadcasted_iota(I32, (256, 128), 1).astype(F32)
    select = jnp.concatenate(
        [jnp.where(row_col == lane + 128.0 * j, 1.0, 0.0).astype(BF16) for j in range(rows_dev // 128)], axis=1
    )
    pay[...] = mm(select, xhi[...]) + mm(select, xlo[...])
    there = pl.ds(pl.multiple_of((1 - c) * 128, 128), 128)
    here = pl.ds(pl.multiple_of(c * 128, 128), 128)
    send("pc", pay.at[there, :], rc, pc_s.at[0], pc_r.at[0], to_c, rc)

    def on_in_y(name, buf, s_sem, r_sem, which, at):
        first, last = RANGES[which]
        part = pl.ds(first, last - first)
        for k in (2, 1, 3):
            send((name, which), buf.at[part, y, c], buf.at[part, y, c], s_sem.at[at, k], r_sem.at[at, k],
                 to_y[k], buf.at[part, yp(NY - k), c])

    def on_to_core(name, buf, s_sem, r_sem, which, at):
        first, last = RANGES[which]
        part = pl.ds(first, last - first)
        send((name, which), buf.at[part, :, c], buf.at[part, :, c], s_sem.at[at], r_sem.at[at], to_c,
             buf.at[part, :, 1 - c])

    arrive("pc")
    b1[...] = pay[here, :] + rc[...]
    for k in (2, 1, 3):
        src = b1.at[pl.ds(pl.multiple_of(yp(k) * 32, 32), 32), :]
        send("py", src, ry.at[k], py_s.at[k], py_r.at[k], to_y[k], ry.at[k])
    arrive(("uz", 1), ("uz", 2), ("uz", 3), ("uz", 4))
    send("up", g.at[pl.ds(1, 4), y, c], g.at[pl.ds(5, 4), y, c], ub_s.at[0], ub_r.at[0], to_z[12],
         g.at[pl.ds(5, 4), y, c])
    arrive(("uz", 15), ("uz", 14), ("uz", 13), ("uz", 12))
    send("down", g.at[pl.ds(13, 3), y, c], g.at[pl.ds(9, 3), y, c], ub_s.at[1], ub_r.at[1], to_z[4],
         g.at[pl.ds(9, 3), y, c])
    on_in_y("uy", g, uy_s, uy_r, "low", 0)
    on_in_y("uy", g, uy_s, uy_r, "high", 1)

    arrive("py")
    b2[...] = b1[pl.ds(pl.multiple_of(y * 32, 32), 32), :] + ry[1] + ry[2] + ry[3]
    for zz in range(NZ):
        for j in range(5):
            sz[zz, j] = b2[2 * zz : 2 * zz + 2, 128 * j : 128 * j + 128]
    arrive("up")
    on_in_y("uy", g, uy_s, uy_r, "up", 2)
    arrive("down")
    on_in_y("uy", g, uy_s, uy_r, "down", 3)
    for k in FAR_FIRST:
        send("pz", sz.at[zp(k)], rz.at[k], pz_s.at[k], pz_r.at[k], to_z[k], rz.at[k])

    arrive(("uy", "low"))
    on_to_core("uc", g, uc_s, uc_r, "low", 0)
    arrive(("uy", "high"))
    on_to_core("uc", g, uc_s, uc_r, "high", 1)
    arrive(("uy", "up"))
    on_to_core("uc", g, uc_s, uc_r, "up", 2)
    arrive(("uy", "down"))
    on_to_core("uc", g, uc_s, uc_r, "down", 3)
    for k in FAR_FIRST:
        at = NZ - k
        send("lz", lp.at[0, y, c], lp.at[at, y, c], lz_s.at[k], lz_r.at[k], to_z[k], lp.at[at, y, c])

    arrive(("uc", "low"), ("uc", "high"), ("uc", "up"), ("uc", "down"))
    flat = g.reshape(NZ * NY * NC * 8, 128)

    @pl.loop(0, NZ)
    def _(k):
        rows = pl.ds(pl.multiple_of(((z + k) % NZ) * 32, 32), 32)
        for h in range(2):
            hi, lo = halves(flat[pl.ds(k * 64 + h, 32, stride=2), :])
            uhi[rows, 128 * h : 128 * h + 128] = hi
            ulo[rows, 128 * h : 128 * h + 128] = lo

    @pl.loop(0, NX)
    def _(part):
        rows = pl.ds(pl.multiple_of(part * quarter, quarter), quarter)
        left, right = xhi[rows, :512], uhi[...]
        prod[rows, :] = mm(left, right) + (mm(xlo[rows, :512], right) + mm(left, ulo[...]))

    def to_owner(k):
        src = prod.at[pl.ds(pl.multiple_of(xp(k) * quarter, quarter), quarter), :]
        send("rx", src, xr.at[k], rx_s.at[k], rx_r.at[k], to_x[k], xr.at[k])

    to_owner(1)
    to_owner(3)

    mine2 = sz[z]
    arrive("pz")
    for k in range(1, NZ):
        mine2 = mine2 + rz[k]
    two = jnp.concatenate([mine2[j] for j in range(4)], axis=1)
    two_hi = two.astype(BF16).astype(F32)
    stacked = jnp.concatenate([two_hi, two - two_hi, jnp.zeros((12, 512), F32)], axis=0).astype(BF16)
    by_hi = mm(stacked, uhi[...])
    by_lo = mm(stacked, ulo[...])
    two = by_hi[0:2] + (by_hi[2:4] + by_lo[0:2])
    for h in range(2):
        xb[x, 2 * h : 2 * h + 2, :] = jnp.where(x == h, mine2[4], 0.0) - two[:, 128 * h : 128 * h + 128]
    for k in (2, 1, 3):
        send("x", xb.at[x], xb.at[x], x_s.at[k], x_r.at[k], to_x[k], xb.at[xp(NX - k)])

    arrive("x")
    w[0, y, c] = xb[0] + xb[1] + xb[2] + xb[3]
    for k in FAR_FIRST:
        at = NZ - k
        send(("wz", at), w.at[0, y, c], w.at[at, y, c], wz_s.at[k], wz_r.at[k], to_z[k], w.at[at, y, c])
    to_owner(2)

    arrive("lz")
    for k in (2, 1, 3):
        send("ly", lp.at[:, y, c], lp.at[:, y, c], ly_s.at[k], ly_r.at[k], to_y[k], lp.at[:, yp(NY - k), c])
    arrive(*[("wz", at) for at in (1, 15, 2, 14, 3, 13, 4, 12)])
    on_in_y("wy", w, wy_s, wy_r, "low", 0)
    on_in_y("wy", w, wy_s, wy_r, "high", 1)
    arrive(*[("wz", at) for at in (5, 11, 6, 10, 7, 9, 8)])
    on_in_y("wy", w, wy_s, wy_r, "up", 2)
    on_in_y("wy", w, wy_s, wy_r, "down", 3)
    arrive("ly")
    send("lc", lp.at[:, :, c], lp.at[:, :, c], lc_s.at[0], lc_r.at[0], to_c, lp.at[:, :, 1 - c])
    arrive(("wy", "low"))
    on_to_core("wc", w, wc_s, wc_r, "low", 0)
    arrive(("wy", "high"))
    on_to_core("wc", w, wc_s, wc_r, "high", 1)
    arrive(("wy", "up"))
    on_to_core("wc", w, wc_s, wc_r, "up", 2)
    arrive(("wy", "down"))
    on_to_core("wc", w, wc_s, wc_r, "down", 3)

    arrive("lc")
    for slot in range(NZ * NY * NC):
        zz, yy, cc = slot // (NY * NC), slot // NC % NY, slot % NC
        for h in range(2):
            lpm[h, slot : slot + 1, :] = lp[(zz - z + NZ) % NZ, yy, cc, :, 128 * h : 128 * h + 128]
    for s in range(2):
        number = rows_dev * blocks[s] + looked_up(lpm, 0, 1, 128, blocks[s], places[s]).astype(I32)
        piv_ref[:, 128 * s : 128 * s + 128] = number[0:1]

    arrive("rx")
    xs[pl.ds(256, quarter), :] = own[...] - (prod[pl.ds(mine, quarter), :] + xr[1] + xr[2] + xr[3])

    arrive(("wc", "low"), ("wc", "high"), ("wc", "up"), ("wc", "down"))
    for slot in range(NC * NY * NZ):
        cc, yy, zz = slot // (NY * NZ), slot // NZ % NY, slot % NZ
        for h in range(2):
            piece = w[(zz - z + NZ) % NZ, yy, cc, 2 * h : 2 * h + 2, :]
            xs[2 * slot : 2 * slot + 2, 128 * h : 128 * h + 128] = piece

    for copy in sends:
        copy.wait_send()


def factor(xs, dinv, piv_in, low_ref, up_ref, piv_ref):
    piv_ref[...] = piv_in[...]
    column = lax.broadcasted_iota(I32, (64, 256), 1)
    pivots, rest = xs[:256], xs[256:]
    for t in range(4):
        inverse = dinv[t]
        u_t = pivots[:64]
        up_ref[64 * t : 64 * t + 64, :] = jnp.where(column >= 64 * t, u_t, 0.0)
        panel = rest[:, 64 * t : 64 * t + 64]
        low_ref[:, 64 * t : 64 * t + 64] = mm3(panel, inverse)
        if t < 3:
            step = mm3(inverse, jnp.where(column >= 64 * (t + 1), u_t, 0.0))
            pivots = pivots[64:] - mm3(pivots[64:, 64 * t : 64 * t + 64], step)
            rest = rest - mm3(panel, step)


def in_hbm(array):
    return pltpu.with_memory_space_constraint(array, pltpu.HBM)


def body(block_column, l_panels, u_blocks, diag_inverses, leaf_pick, merge_pick, final_order):
    rows_dev, cols = block_column.shape
    quarter = rows_dev // NX
    vmem = pl.BlockSpec(memory_space=pltpu.VMEM)
    sem = pltpu.SemaphoreType.DMA
    xs, piv = pl.pallas_call(
        kernel,
        name="panel",
        out_shape=(jax.ShapeDtypeStruct((256 + quarter, cols), F32), jax.ShapeDtypeStruct((1, cols), I32)),
        in_specs=[pl.BlockSpec(memory_space=pltpu.HBM)] * 6,
        out_specs=(vmem, vmem),
        scratch_shapes=[
            pltpu.VMEM((rows_dev * 4, 128), F32),
            pltpu.VMEM((rows_dev, 128), F32),
            pltpu.VMEM((quarter, cols), F32),
            pltpu.VMEM((1, 256), I32),
            pltpu.VMEM((2, 128, 128), I32),
            pltpu.VMEM((1, 256), I32),
            pltpu.VMEM((4, 256), F32),
            pltpu.VMEM((rows_dev, 640), BF16),
            pltpu.VMEM((rows_dev, 640), BF16),
            pltpu.VMEM((NZ, NY, NC, 8, 128), F32),
            pltpu.VMEM((NZ, NY, NC, 1, 256), I32),
            pltpu.VMEM((2, 128, 128), I32),
            pltpu.VMEM((256, 640), F32),
            pltpu.VMEM((128, 640), F32),
            pltpu.VMEM((128, 640), F32),
            pltpu.VMEM((NY, 32, 640), F32),
            pltpu.VMEM((32, 640), F32),
            pltpu.VMEM((NZ, 5, 2, 128), F32),
            pltpu.VMEM((NZ, 5, 2, 128), F32),
            pltpu.VMEM((512, cols), BF16),
            pltpu.VMEM((512, cols), BF16),
            pltpu.VMEM((rows_dev, cols), F32),
            pltpu.VMEM((NX, quarter, cols), F32),
            pltpu.VMEM((NX, 4, 128), F32),
            pltpu.VMEM((NZ, NY, NC, 4, 128), F32),
            sem((8,)),
            sem((NZ,)), sem((NZ,)), sem((2,)), sem((2,)), sem((4, NY)), sem((4, NY)), sem((4,)), sem((4,)),
            sem((NZ,)), sem((NZ,)), sem((NY,)), sem((NY,)), sem((1,)), sem((1,)),
            sem((1,)), sem((1,)), sem((NY,)), sem((NY,)), sem((NZ,)), sem((NZ,)),
            sem((NX,)), sem((NX,)),
            sem((NZ,)), sem((NZ,)), sem((4, NY)), sem((4, NY)), sem((4,)), sem((4,)),
            sem((NX,)), sem((NX,)),
        ],
        compiler_params=pltpu.CompilerParams(
            collective_id=0, has_side_effects=True, vmem_limit_bytes=24 * 1024 * 1024
        ),
    )(
        in_hbm(l_panels.reshape(-1, 128)),
        in_hbm(block_column),
        in_hbm(u_blocks[0]),
        in_hbm(leaf_pick),
        in_hbm(merge_pick),
        in_hbm(final_order.reshape(1, -1)),
    )
    low, up, piv = pl.pallas_call(
        factor,
        name="factor",
        out_shape=(
            jax.ShapeDtypeStruct((quarter, cols), F32),
            jax.ShapeDtypeStruct((cols, cols), F32),
            jax.ShapeDtypeStruct((1, cols), I32),
        ),
        in_specs=[vmem] * 3,
        out_specs=(vmem,) * 3,
        compiler_params=pltpu.CompilerParams(vmem_limit_bytes=8 * 1024 * 1024),
    )(xs, diag_inverses, piv)
    return low, up, piv[0]


def solution(mesh):
    return jax.shard_map(
        body,
        mesh=mesh,
        in_specs=(
            P("rows", None),
            P("rows", None, "panels", None),
            P("panels", "rows", None),
            P(),
            P("rows", None),
            P(),
            P(),
        ),
        out_specs=(P(("rows", "panels"), None), P(), P()),
        check_vma=False,
    )
```

```python
import functools

import jax
import jax.numpy as jnp
from jax import lax
from jax.experimental import pallas as pl
from jax.experimental.pallas import tpu as pltpu
from jax.sharding import PartitionSpec as P

MESH = pl.DeviceIdType.MESH
F32, BF16, I32 = jnp.float32, jnp.bfloat16, jnp.int32
NZ, NY, NC, NX = 16, 4, 2, 4
FAR_FIRST = (8, 7, 9, 6, 10, 5, 11, 4, 12, 3, 13, 2, 14, 1, 15)
NEAR = (4, 12, 3, 13, 2, 14, 1, 15)
RANGES = {"low": (0, 5), "high": (12, 16), "up": (5, 9), "down": (9, 12),
          "w_low": (0, 6), "w_high": (11, 16), "w_far": (6, 11)}


def halves(v):
    hi = v.astype(BF16)
    return hi, (v - hi.astype(F32)).astype(BF16)


def mm(a, b):
    return jnp.dot(a, b, preferred_element_type=F32)


def mm3(a, b):
    ah, al = halves(a)
    bh, bl = halves(b)
    return mm(ah, bh) + (mm(al, bh) + mm(ah, bl))


def kernel(
    l_hbm, bc_hbm, u_hbm, leaf_hbm, mp_hbm, fo_hbm,
    xs, piv_ref,
    l_raw, aux_raw, own, leaf, mp, fo, u_raw, rv, rs,
    xhi, xlo, g, lp, lpm, give, keep, rc, ry, b2, sz, rz, uhi, ulo, prod, xr, xb, w,
    in_sem, uz_s, uz_r, ub_s, ub_r, uy_s, uy_r, uc_s, uc_r, lz_s, lz_r, ly_s, ly_r, lc_s, lc_r,
    pc_s, pc_r, py_s, py_r, pz_s, pz_r, x_s, x_r, wz_s, wz_r, wy_s, wy_r, wc_s, wc_r, rx_s, rx_r,
):
    row = lax.axis_index("rows")
    x = lax.axis_index("panels")
    z, y, c = row // (NY * NC), (row // NC) % NY, row % NC
    rows_dev = bc_hbm.shape[0]
    quarter = rows_dev // NX

    def dev(zz, yy, cc, xx):
        return ((zz * NY + yy) * NC + cc, xx)

    def zp(k):
        return (z + k) % NZ

    def yp(k):
        return (y + k) % NY

    def xp(k):
        return (x + k) % NX

    to_z = [dev(zp(k), y, c, x) for k in range(NZ)]
    to_y = [dev(z, yp(k), c, x) for k in range(NY)]
    to_x = [dev(z, y, c, xp(k)) for k in range(NX)]
    to_c = dev(z, y, 1 - c, x)

    col = pl.multiple_of((x % 2) * 128, 128)
    mine = pl.multiple_of(x * quarter, quarter)
    loads = [
        pltpu.make_async_copy(mp_hbm.at[:, pl.ds(0, 128)], mp.at[0], in_sem.at[0]),
        pltpu.make_async_copy(fo_hbm, fo, in_sem.at[1]),
        pltpu.make_async_copy(leaf_hbm, leaf, in_sem.at[2]),
        pltpu.make_async_copy(u_hbm, u_raw, in_sem.at[3]),
        pltpu.make_async_copy(mp_hbm.at[:, pl.ds(128, 128)], mp.at[1], in_sem.at[7]),
        pltpu.make_async_copy(l_hbm, l_raw.at[pl.ds(0, 4 * rows_dev), :], in_sem.at[4]),
        pltpu.make_async_copy(bc_hbm.at[:, pl.ds(col, 128)], aux_raw.at[pl.ds(0, rows_dev), :], in_sem.at[5]),
        pltpu.make_async_copy(bc_hbm.at[pl.ds(mine, quarter), :], own, in_sem.at[6]),
    ]
    for copy in loads:
        copy.start()

    l_raw[4 * rows_dev :, :] = jnp.zeros((8, 128), F32)
    aux_raw[rows_dev:, :] = jnp.zeros((8, 128), F32)

    barrier = pltpu.get_barrier_semaphore()
    partners = [to_z[k] for k in NEAR] + to_y[1:] + to_x[1:] + [to_c]
    for partner in partners:
        pl.semaphore_signal(barrier, inc=1, device_id=partner, device_id_type=MESH)

    sends = []
    arrivals = {}

    def send(name, src, dst, send_sem, recv_sem, to, lands):
        copy = pltpu.make_async_remote_copy(src, dst, send_sem, recv_sem, device_id=to, device_id_type=MESH)
        copy.start()
        sends.append(copy)
        came = pltpu.make_async_remote_copy(lands, lands, send_sem, recv_sem, device_id=to, device_id_type=MESH)
        arrivals.setdefault(name, []).append(came)

    def arrive(*names):
        for name in names:
            for copy in arrivals.pop(name)[::-1]:
                copy.wait_recv()

    for copy in loads[3:4]:
        copy.wait()
    for i in range(4):
        for h in range(2):
            g[0, y, c, 2 * i + h : 2 * i + h + 1, :] = u_raw[i : i + 1, 128 * h : 128 * h + 128]

    for copy in loads[:3] + loads[4:5]:
        copy.wait()
    lp[0, y, c] = leaf[...]
    down = lax.broadcasted_iota(I32, (8, 128), 0)

    def picked(half0, half1, at):
        low = at & 127
        return jnp.where(at >= 128, jnp.take_along_axis(half1, low, axis=1), jnp.take_along_axis(half0, low, axis=1))

    def looked_up(table, first, stride, count, owner, at):
        if count < 8:
            total = jnp.zeros((8, 128), F32)
            for i in range(count):
                line = first + i * stride
                rows = [jnp.broadcast_to(table[h, line : line + 1, :], (8, 128)) for h in range(2)]
                total = jnp.where(owner == i, picked(*rows, at).astype(F32), total)
            return total
        total = jnp.zeros((8, 128), F32)
        for i in range(0, count, 8):
            rows = [table[h, pl.ds(first + i * stride, 8, stride=stride), :] for h in range(2)]
            total += jnp.where(owner - i == down, picked(*rows, at).astype(F32), 0.0)
        return jnp.broadcast_to(jnp.sum(total, axis=0, keepdims=True), (8, 128))

    blocks, places = [], []
    for s in range(2):
        at = jnp.broadcast_to(fo[:, 128 * s : 128 * s + 128], (8, 128))
        block = jnp.zeros((8, 128), I32)
        for level in reversed(range(7)):
            found = looked_up(mp, 1 << level, 2 << level, 64 >> level, block, at).astype(I32)
            block = 2 * block + (found >> 8)
            at = found & 255
        rows = [jnp.broadcast_to(leaf[:, 128 * h : 128 * h + 128], (8, 128)) for h in range(2)]
        blocks.append(block)
        places.append(at)
        rv[:, 128 * s : 128 * s + 128] = jnp.where(block == row, picked(*rows, at), rows_dev)[0:1]
    to_scalars = pltpu.make_async_copy(rv, rs, in_sem.at[8])
    to_scalars.start()

    pl.semaphore_wait(barrier, len(partners))
    for k in NEAR:
        at = NZ - k
        send(("uz", at), g.at[0, y, c], g.at[at, y, c], uz_s.at[k], uz_r.at[k], to_z[k], g.at[at, y, c])

    to_scalars.wait()
    for copy in loads[5:]:
        copy.wait()
    y_order = (2, 1, 3, 0)

    def gather(into, core, k):
        base = core * 128 + yp(k) * 32
        for i in range(32):
            at = rs[0, base + i]
            for j in range(4):
                into[i : i + 1, 128 * j : 128 * j + 128] = l_raw[pl.ds(4 * at + j, 1), :]
            into[i : i + 1, 512:640] = aux_raw[pl.ds(jnp.where(x < 2, at, rows_dev), 1), :]

    for k in y_order:
        gather(give.at[k], 1 - c, k)
        send(("pc", k), give.at[k], rc.at[k], pc_s.at[k], pc_r.at[k], to_c, rc.at[k])
    for k in y_order:
        gather(keep.at[k], c, k)

    def on_in_y(name, buf, s_sem, r_sem, which, at):
        first, last = RANGES[which]
        part = pl.ds(first, last - first)
        for k in (2, 1, 3):
            send((name, which), buf.at[part, y, c], buf.at[part, y, c], s_sem.at[at, k], r_sem.at[at, k],
                 to_y[k], buf.at[part, yp(NY - k), c])

    def on_to_core(name, buf, s_sem, r_sem, which, at):
        first, last = RANGES[which]
        part = pl.ds(first, last - first)
        send((name, which), buf.at[part, :, c], buf.at[part, :, c], s_sem.at[at], r_sem.at[at], to_c,
             buf.at[part, :, 1 - c])

    for k in y_order[:3]:
        arrive(("pc", k))
        keep[k] = keep[k] + rc[k]
        send("py", keep.at[k], ry.at[k], py_s.at[k], py_r.at[k], to_y[k], ry.at[k])
    arrive(("pc", 0))
    arrive(("uz", 1), ("uz", 2), ("uz", 3), ("uz", 4))
    send("up", g.at[pl.ds(1, 4), y, c], g.at[pl.ds(5, 4), y, c], ub_s.at[0], ub_r.at[0], to_z[12],
         g.at[pl.ds(5, 4), y, c])
    arrive(("uz", 15), ("uz", 14), ("uz", 13), ("uz", 12))
    send("down", g.at[pl.ds(13, 3), y, c], g.at[pl.ds(9, 3), y, c], ub_s.at[1], ub_r.at[1], to_z[4],
         g.at[pl.ds(9, 3), y, c])
    on_in_y("uy", g, uy_s, uy_r, "low", 0)
    on_in_y("uy", g, uy_s, uy_r, "high", 1)

    for part in range(NX):
        rows = pl.ds(part * quarter, quarter)
        for j in range(4):
            hi, lo = halves(l_raw[pl.ds(part * quarter * 4 + j, quarter, stride=4), :])
            xhi[rows, 128 * j : 128 * j + 128] = hi
            xlo[rows, 128 * j : 128 * j + 128] = lo

    arrive("py")
    b2[...] = keep[0] + rc[0] + ry[1] + ry[2] + ry[3]
    for zz in range(NZ):
        for j in range(5):
            sz[zz, j] = b2[2 * zz : 2 * zz + 2, 128 * j : 128 * j + 128]
    for k in FAR_FIRST:
        send("pz", sz.at[zp(k)], rz.at[k], pz_s.at[k], pz_r.at[k], to_z[k], rz.at[k])
    arrive("up")
    on_in_y("uy", g, uy_s, uy_r, "up", 2)
    arrive("down")
    on_in_y("uy", g, uy_s, uy_r, "down", 3)
    arrive(("uy", "low"))
    on_to_core("uc", g, uc_s, uc_r, "low", 0)
    arrive(("uy", "high"))
    on_to_core("uc", g, uc_s, uc_r, "high", 1)
    arrive(("uy", "up"))
    on_to_core("uc", g, uc_s, uc_r, "up", 2)
    arrive(("uy", "down"))
    on_to_core("uc", g, uc_s, uc_r, "down", 3)
    arrive(("uc", "low"), ("uc", "high"), ("uc", "up"), ("uc", "down"))
    flat = g.reshape(NZ * NY * NC * 8, 128)

    @pl.loop(0, NZ)
    def _(k):
        rows = pl.ds(pl.multiple_of(((z + k) % NZ) * 32, 32), 32)
        for h in range(2):
            hi, lo = halves(flat[pl.ds(k * 64 + h, 32, stride=2), :])
            uhi[rows, 128 * h : 128 * h + 128] = hi
            ulo[rows, 128 * h : 128 * h + 128] = lo

    mine2 = sz[z]
    arrive("pz")
    for k in range(1, NZ):
        mine2 = mine2 + rz[k]
    two = jnp.concatenate([mine2[j] for j in range(4)], axis=1)
    two_hi = two.astype(BF16).astype(F32)
    stacked = jnp.concatenate([two_hi, two - two_hi, jnp.zeros((12, 512), F32)], axis=0).astype(BF16)
    by_hi = mm(stacked, uhi[...])
    by_lo = mm(stacked, ulo[...])
    two = by_hi[0:2] + (by_hi[2:4] + by_lo[0:2])
    for h in range(2):
        xb[x, 2 * h : 2 * h + 2, :] = jnp.where(x == h, mine2[4], 0.0) - two[:, 128 * h : 128 * h + 128]
    for k in (2, 1, 3):
        send("x", xb.at[x], xb.at[x], x_s.at[k], x_r.at[k], to_x[k], xb.at[xp(NX - k)])

    half = quarter // 2

    def partial(k):
        for h in range(2):
            rows = pl.ds(pl.multiple_of(xp(k) * quarter + h * half, half), half)
            left, right = xhi[rows, :], uhi[...]
            prod[k, h] = mm(left, right) + (mm(xlo[rows, :], right) + mm(left, ulo[...]))

    def to_neighbour(name, k, src, at):
        send((name, k), src, xr.at[at], rx_s.at[at], rx_r.at[at], to_x[k], xr.at[at])

    partial(2)
    to_neighbour("relay", 1, prod.at[2, 0], 0)
    to_neighbour("relay", 3, prod.at[2, 1], 1)
    partial(1)
    to_neighbour("rx", 1, prod.at[1, 1], 2)
    partial(3)
    to_neighbour("rx", 3, prod.at[3, 0], 3)
    partial(0)
    for k in FAR_FIRST:
        at = NZ - k
        send("lz", lp.at[0, y, c], lp.at[at, y, c], lz_s.at[k], lz_r.at[k], to_z[k], lp.at[at, y, c])

    arrive("x")
    w[0, y, c] = xb[0] + xb[1] + xb[2] + xb[3]
    def far(k):
        for j in (2, 1, 3, 0):
            send(("wf", j), w.at[0, y, c], w.at[NZ - k, y, c], wz_s.at[k, j], wz_r.at[k, j],
                 dev(zp(k), yp(j), c, x), w.at[NZ - k, yp(NY - j), c])

    def near(k):
        at = NZ - k
        send(("wz", at), w.at[0, y, c], w.at[at, y, c], wz_s.at[k, 0], wz_r.at[k, 0], to_z[k], w.at[at, y, c])

    for step, k in ((far, 8), (far, 7), (far, 9), (near, 5), (near, 11), (far, 6), (far, 10)):
        step(k)
    for k in NEAR:
        near(k)

    arrive(("relay", 1))
    prod[1, 0] = prod[1, 0] + xr[0]
    to_neighbour("rx2", 1, prod.at[1, 0], 4)
    arrive(("relay", 3))
    prod[3, 1] = prod[3, 1] + xr[1]
    to_neighbour("rx2", 3, prod.at[3, 1], 5)
    arrive(*[("wz", at) for at in (1, 2, 3, 4, 5)])
    on_in_y("wy", w, wy_s, wy_r, "w_low", 0)
    arrive(*[("wz", at) for at in (15, 14, 13, 12, 11)])
    on_in_y("wy", w, wy_s, wy_r, "w_high", 1)
    arrive("lz")
    for k in (2, 1, 3):
        send("ly", lp.at[:, y, c], lp.at[:, y, c], ly_s.at[k], ly_r.at[k], to_y[k], lp.at[:, yp(NY - k), c])

    arrive(("wy", "w_low"))
    on_to_core("wc", w, wc_s, wc_r, "w_low", 0)
    arrive(("wy", "w_high"))
    on_to_core("wc", w, wc_s, wc_r, "w_high", 1)
    arrive(("wf", 0), ("wf", 1), ("wf", 3), ("wf", 2))
    on_to_core("wc", w, wc_s, wc_r, "w_far", 2)
    arrive("ly")
    send("lc", lp.at[:, :, c], lp.at[:, :, c], lc_s.at[0], lc_r.at[0], to_c, lp.at[:, :, 1 - c])
    arrive("lc")
    for slot in range(NZ * NY * NC):
        zz, yy, cc = slot // (NY * NC), slot // NC % NY, slot % NC
        for h in range(2):
            lpm[h, slot : slot + 1, :] = lp[(zz - z + NZ) % NZ, yy, cc, :, 128 * h : 128 * h + 128]
    for s in range(2):
        number = rows_dev * blocks[s] + looked_up(lpm, 0, 1, 128, blocks[s], places[s]).astype(I32)
        piv_ref[:, 128 * s : 128 * s + 128] = number[0:1]
    arrive(("rx", 1), ("rx", 3), ("rx2", 1), ("rx2", 3))
    xs[256 : 256 + half, :] = own[:half, :] - (prod[0, 0] + xr[3] + xr[4])
    xs[256 + half :, :] = own[half:, :] - (prod[0, 1] + xr[2] + xr[5])

    arrive(("wc", "w_low"), ("wc", "w_high"), ("wc", "w_far"))
    for slot in range(NC * NY * NZ):
        cc, yy, zz = slot // (NY * NZ), slot // NZ % NY, slot % NZ
        for h in range(2):
            piece = w[(zz - z + NZ) % NZ, yy, cc, 2 * h : 2 * h + 2, :]
            xs[2 * slot : 2 * slot + 2, 128 * h : 128 * h + 128] = piece

    for copy in sends:
        copy.wait_send()


def factor(xs, dinv, piv_in, low_ref, up_ref, piv_ref):
    piv_ref[...] = piv_in[...]
    column = lax.broadcasted_iota(I32, (64, 256), 1)
    pivots, rest = xs[:256], xs[256:]
    for t in range(4):
        inverse = dinv[t]
        u_t = pivots[:64]
        up_ref[64 * t : 64 * t + 64, :] = jnp.where(column >= 64 * t, u_t, 0.0)
        panel = rest[:, 64 * t : 64 * t + 64]
        low_ref[:, 64 * t : 64 * t + 64] = mm3(panel, inverse)
        if t < 3:
            step = mm3(inverse, jnp.where(column >= 64 * (t + 1), u_t, 0.0))
            pivots = pivots[64:] - mm3(pivots[64:, 64 * t : 64 * t + 64], step)
            rest = rest - mm3(panel, step)


def in_hbm(array):
    return pltpu.with_memory_space_constraint(array, pltpu.HBM)


def body(block_column, l_panels, u_blocks, diag_inverses, leaf_pick, merge_pick, final_order):
    rows_dev, cols = block_column.shape
    quarter = rows_dev // NX
    vmem = pl.BlockSpec(memory_space=pltpu.VMEM)
    sem = pltpu.SemaphoreType.DMA
    xs, piv = pl.pallas_call(
        kernel,
        name="panel",
        out_shape=(jax.ShapeDtypeStruct((256 + quarter, cols), F32), jax.ShapeDtypeStruct((1, cols), I32)),
        in_specs=[pl.BlockSpec(memory_space=pltpu.HBM)] * 6,
        out_specs=(vmem, vmem),
        scratch_shapes=[
            pltpu.VMEM((rows_dev * 4 + 8, 128), F32),
            pltpu.VMEM((rows_dev + 8, 128), F32),
            pltpu.VMEM((quarter, cols), F32),
            pltpu.VMEM((1, 256), I32),
            pltpu.VMEM((2, 128, 128), I32),
            pltpu.VMEM((1, 256), I32),
            pltpu.VMEM((4, 256), F32),
            pltpu.VMEM((1, 256), I32),
            pltpu.SMEM((1, 256), I32),
            pltpu.VMEM((rows_dev, 512), BF16),
            pltpu.VMEM((rows_dev, 512), BF16),
            pltpu.VMEM((NZ, NY, NC, 8, 128), F32),
            pltpu.VMEM((NZ, NY, NC, 1, 256), I32),
            pltpu.VMEM((2, 128, 128), I32),
            pltpu.VMEM((NY, 32, 640), F32),
            pltpu.VMEM((NY, 32, 640), F32),
            pltpu.VMEM((NY, 32, 640), F32),
            pltpu.VMEM((NY, 32, 640), F32),
            pltpu.VMEM((32, 640), F32),
            pltpu.VMEM((NZ, 5, 2, 128), F32),
            pltpu.VMEM((NZ, 5, 2, 128), F32),
            pltpu.VMEM((512, cols), BF16),
            pltpu.VMEM((512, cols), BF16),
            pltpu.VMEM((NX, 2, quarter // 2, cols), F32),
            pltpu.VMEM((6, quarter // 2, cols), F32),
            pltpu.VMEM((NX, 4, 128), F32),
            pltpu.VMEM((NZ, NY, NC, 4, 128), F32),
            sem((9,)),
            sem((NZ,)), sem((NZ,)), sem((2,)), sem((2,)), sem((4, NY)), sem((4, NY)), sem((4,)), sem((4,)),
            sem((NZ,)), sem((NZ,)), sem((NY,)), sem((NY,)), sem((1,)), sem((1,)),
            sem((NY,)), sem((NY,)), sem((NY,)), sem((NY,)), sem((NZ,)), sem((NZ,)),
            sem((NX,)), sem((NX,)),
            sem((NZ, NY)), sem((NZ, NY)), sem((4, NY)), sem((4, NY)), sem((4,)), sem((4,)),
            sem((6,)), sem((6,)),
        ],
        compiler_params=pltpu.CompilerParams(
            collective_id=0, has_side_effects=True, vmem_limit_bytes=24 * 1024 * 1024
        ),
    )(
        in_hbm(l_panels.reshape(-1, 128)),
        in_hbm(block_column),
        in_hbm(u_blocks[0]),
        in_hbm(leaf_pick),
        in_hbm(merge_pick),
        in_hbm(final_order.reshape(1, -1)),
    )
    low, up, piv = pl.pallas_call(
        factor,
        name="factor",
        out_shape=(
            jax.ShapeDtypeStruct((quarter, cols), F32),
            jax.ShapeDtypeStruct((cols, cols), F32),
            jax.ShapeDtypeStruct((1, cols), I32),
        ),
        in_specs=[vmem] * 3,
        out_specs=(vmem,) * 3,
        compiler_params=pltpu.CompilerParams(vmem_limit_bytes=8 * 1024 * 1024),
    )(xs, diag_inverses, piv)
    return low, up, piv[0]


def solution(mesh):
    return jax.shard_map(
        body,
        mesh=mesh,
        in_specs=(
            P("rows", None),
            P("rows", None, "panels", None),
            P("panels", "rows", None),
            P(),
            P("rows", None),
            P(),
            P(),
        ),
        out_specs=(P(("rows", "panels"), None), P(), P()),
        check_vma=False,
    )
```

```python
import functools

import jax
import jax.numpy as jnp
from jax import lax
from jax.experimental import pallas as pl
from jax.experimental.pallas import tpu as pltpu
from jax.sharding import PartitionSpec as P

MESH = pl.DeviceIdType.MESH
F32, BF16, I32 = jnp.float32, jnp.bfloat16, jnp.int32
NZ, NY, NC, NX = 16, 4, 2, 4
FAR_FIRST = (8, 7, 9, 6, 10, 5, 11, 4, 12, 3, 13, 2, 14, 1, 15)
CLOSE = (3, 13, 2, 14, 1, 15)
NEAR = (4, 12) + CLOSE
RANGES = {"low": (0, 4), "high": (13, 16), "up": (4, 7), "down": (10, 13), "far": (7, 10),
          "w_low": (0, 6), "w_high": (11, 16), "w_far": (6, 11)}


def halves(v):
    hi = v.astype(BF16)
    return hi, (v - hi.astype(F32)).astype(BF16)


def mm(a, b):
    return jnp.dot(a, b, preferred_element_type=F32)


def mm3(a, b):
    ah, al = halves(a)
    bh, bl = halves(b)
    return mm(jnp.concatenate([ah, al], axis=1), jnp.concatenate([bh, bh], axis=0)) + mm(ah, bl)


def kernel(
    l_hbm, bc_hbm, u_hbm, leaf_hbm, mp_hbm, fo_hbm,
    xs, rows_ref, first_ref,
    l_raw, aux_raw, own, leaf, mp, fo, u_raw, rv, rs,
    xhi, xlo, g, give, keep, rc, ry, b2, sz, rz, uhi, ulo, prod, xr, xb, w, ids,
    in_sem, known, uz_s, uz_r, ub_s, ub_r, uy_s, uy_r, uc_s, uc_r,
    pc_s, pc_r, py_s, py_r, pz_s, pz_r, x_s, x_r, wz_s, wz_r, wy_s, wy_r, wc_s, wc_r, rx_s, rx_r,
    iz_s, iz_r, iy_s, iy_r, ic_s, ic_r,
):
    row = lax.axis_index("rows")
    x = lax.axis_index("panels")
    z, y, c = row // (NY * NC), (row // NC) % NY, row % NC
    rows_dev = bc_hbm.shape[0]
    quarter = rows_dev // NX

    def dev(zz, yy, cc, xx):
        return ((zz * NY + yy) * NC + cc, xx)

    def zp(k):
        return (z + k) % NZ

    def yp(k):
        return (y + k) % NY

    def xp(k):
        return (x + k) % NX

    to_z = [dev(zp(k), y, c, x) for k in range(NZ)]
    to_y = [dev(z, yp(k), c, x) for k in range(NY)]
    to_x = [dev(z, y, c, xp(k)) for k in range(NX)]
    to_c = dev(z, y, 1 - c, x)

    col = pl.multiple_of((x // 2) * 128, 128)
    mine = pl.multiple_of(x * quarter, quarter)
    loads = [
        pltpu.make_async_copy(mp_hbm.at[:, pl.ds(0, 128)], mp.at[0], in_sem.at[0]),
        pltpu.make_async_copy(fo_hbm, fo, in_sem.at[1]),
        pltpu.make_async_copy(leaf_hbm, leaf, in_sem.at[2]),
        pltpu.make_async_copy(u_hbm, u_raw, in_sem.at[3]),
        pltpu.make_async_copy(mp_hbm.at[:, pl.ds(128, 128)], mp.at[1], in_sem.at[7]),
        pltpu.make_async_copy(l_hbm, l_raw.at[pl.ds(0, 4 * rows_dev), :], in_sem.at[4]),
        pltpu.make_async_copy(bc_hbm.at[:, pl.ds(col, 128)], aux_raw.at[pl.ds(0, rows_dev), :], in_sem.at[5]),
        pltpu.make_async_copy(bc_hbm.at[pl.ds(mine, quarter), :], own, in_sem.at[6]),
    ]
    for copy in loads:
        copy.start()

    l_raw[4 * rows_dev :, :] = jnp.zeros((8, 128), F32)
    aux_raw[rows_dev:, :] = jnp.zeros((8, 128), F32)

    barrier = pltpu.get_barrier_semaphore()
    partners = [to_z[k] for k in CLOSE] + to_y[1:] + to_x[1:] + [to_c]
    for partner in partners:
        pl.semaphore_signal(barrier, inc=1, device_id=partner, device_id_type=MESH)

    sends = []
    arrivals = {}

    def send(name, src, dst, send_sem, recv_sem, to, lands):
        copy = pltpu.make_async_remote_copy(src, dst, send_sem, recv_sem, device_id=to, device_id_type=MESH)
        copy.start()
        sends.append(copy)
        came = pltpu.make_async_remote_copy(lands, lands, send_sem, recv_sem, device_id=to, device_id_type=MESH)
        arrivals.setdefault(name, []).append(came)

    def arrive(*names):
        for name in names:
            for copy in arrivals.pop(name)[::-1]:
                copy.wait_recv()

    def settle(count):
        for copy in sends[:count]:
            copy.wait_send()
        del sends[:count]

    for copy in loads[3:4]:
        copy.wait()
    for i in range(4):
        for h in range(2):
            g[0, y, c, 2 * i + h : 2 * i + h + 1, :] = u_raw[i : i + 1, 128 * h : 128 * h + 128]

    for copy in loads[:3] + loads[4:5]:
        copy.wait()
    down = lax.broadcasted_iota(I32, (8, 128), 0)

    def picked(half0, half1, at):
        low = at & 127
        return jnp.where(at >= 128, jnp.take_along_axis(half1, low, axis=1), jnp.take_along_axis(half0, low, axis=1))

    def looked_up(table, first, stride, count, owner, at):
        if count < 8:
            total = jnp.zeros((8, 128), F32)
            for i in range(count):
                line = first + i * stride
                rows = [jnp.broadcast_to(table[h, line : line + 1, :], (8, 128)) for h in range(2)]
                total = jnp.where(owner == i, picked(*rows, at).astype(F32), total)
            return total
        total = jnp.zeros((8, 128), F32)
        for i in range(0, count, 8):
            rows = [table[h, pl.ds(first + i * stride, 8, stride=stride), :] for h in range(2)]
            total += jnp.where(owner - i == down, picked(*rows, at).astype(F32), 0.0)
        return jnp.broadcast_to(jnp.sum(total, axis=0, keepdims=True), (8, 128))

    for s in range(2):
        at = jnp.broadcast_to(fo[:, 128 * s : 128 * s + 128], (8, 128))
        block = jnp.zeros((8, 128), I32)
        for level in reversed(range(7)):
            found = looked_up(mp, 1 << level, 2 << level, 64 >> level, block, at).astype(I32)
            block = 2 * block + (found >> 8)
            at = found & 255
        rows = [jnp.broadcast_to(leaf[:, 128 * h : 128 * h + 128], (8, 128)) for h in range(2)]
        first_ref[:, 128 * s : 128 * s + 128] = rows_dev * block[0:1]
        rv[:, 128 * s : 128 * s + 128] = jnp.where(block == row, picked(*rows, at), rows_dev)[0:1]
    to_scalars = pltpu.make_async_copy(rv, rs, in_sem.at[8])
    to_scalars.start()

    pl.semaphore_wait(barrier, len(partners))
    for k in CLOSE:
        at = NZ - k
        send(("uz", at), g.at[0, y, c], g.at[at, y, c], uz_s.at[k], uz_r.at[k], to_z[k], g.at[at, y, c])

    to_scalars.wait()
    for copy in loads[5:]:
        copy.wait()

    quarter_lane = lax.broadcasted_iota(I32, (rows_dev, 128), 1) // 64 == x % 2
    numbers = lax.broadcasted_iota(I32, (rows_dev, 128), 0).astype(F32)
    aux_raw[:rows_dev, :] = jnp.where(quarter_lane, aux_raw[:rows_dev, :], numbers)

    def gather(into, core, k):
        base = core * 128 + yp(k) * 32
        for i in range(32):
            at = rs[0, base + i]
            for j in range(4):
                into[i : i + 1, 128 * j : 128 * j + 128] = l_raw[pl.ds(4 * at + j, 1), :]
            into[i : i + 1, 512:640] = aux_raw[pl.ds(at, 1), :]

    def hand_over(k):
        gather(give.at[k], 1 - c, k)
        send(("pc", k), give.at[k], rc.at[k], pc_s.at[k], pc_r.at[k], to_c, rc.at[k])

    def fold(k):
        gather(keep.at[k], c, k)
        arrive(("pc", k))
        keep[k] = keep[k] + rc[k]
        send("py", keep.at[k], ry.at[k], py_s.at[k], py_r.at[k], to_y[k], ry.at[k])

    hand_over(2)
    hand_over(1)
    fold(2)
    hand_over(3)
    fold(1)
    hand_over(0)
    fold(3)
    gather(keep.at[0], c, 0)
    arrive(("pc", 0))

    def on_in_y(name, buf, s_sem, r_sem, which, at):
        first, last = RANGES[which]
        part = pl.ds(first, last - first)
        for k in (2, 1, 3):
            send((name, which), buf.at[part, y, c], buf.at[part, y, c], s_sem.at[at, k], r_sem.at[at, k],
                 to_y[k], buf.at[part, yp(NY - k), c])

    def on_to_core(name, buf, s_sem, r_sem, which, at):
        first, last = RANGES[which]
        part = pl.ds(first, last - first)
        send((name, which), buf.at[part, :, c], buf.at[part, :, c], s_sem.at[at], r_sem.at[at], to_c,
             buf.at[part, :, 1 - c])

    def second(name, at, k, first, last, there):
        src, dst = pl.ds(first, last - first), pl.ds(there, last - first)
        send(name, g.at[src, y, c], g.at[dst, y, c], ub_s.at[at], ub_r.at[at], to_z[k], g.at[dst, y, c])

    arrive(*[("uz", at) for at in (1, 15, 2, 14, 3, 13)])
    second("far up", 0, 11, 2, 4, 7)
    second("far down", 1, 5, 14, 15, 9)
    second("up", 2, 13, 1, 4, 4)
    second("down", 3, 3, 13, 16, 10)
    for k in (3, 13):
        pl.semaphore_signal(known, inc=1, device_id=to_z[k], device_id_type=MESH)
    on_in_y("uy", g, uy_s, uy_r, "low", 0)
    on_in_y("uy", g, uy_s, uy_r, "high", 1)

    for part in range(NX):
        rows = pl.ds(part * quarter, quarter)
        for j in range(4):
            hi, lo = halves(l_raw[pl.ds(part * quarter * 4 + j, quarter, stride=4), :])
            xhi[rows, 128 * j : 128 * j + 128] = hi
            xlo[rows, 128 * j : 128 * j + 128] = lo

    arrive("py")
    b2[...] = keep[0] + rc[0] + ry[1] + ry[2] + ry[3]
    for zz in range(NZ):
        for j in range(5):
            sz[zz, j] = b2[2 * zz : 2 * zz + 2, 128 * j : 128 * j + 128]
    pl.semaphore_wait(known, 2)
    for k in FAR_FIRST:
        send("pz", sz.at[zp(k)], rz.at[k], pz_s.at[k], pz_r.at[k], to_z[k], rz.at[k])
    arrive("up")
    on_in_y("uy", g, uy_s, uy_r, "up", 2)
    arrive("down")
    on_in_y("uy", g, uy_s, uy_r, "down", 3)
    arrive("far up", "far down")
    on_in_y("uy", g, uy_s, uy_r, "far", 4)
    settle(17)
    arrive(("uy", "low"))
    on_to_core("uc", g, uc_s, uc_r, "low", 0)
    arrive(("uy", "high"))
    on_to_core("uc", g, uc_s, uc_r, "high", 1)
    flat = g.reshape(NZ * NY * NC * 8, 128)

    def rounded(k):
        rows = pl.ds(pl.multiple_of(zp(k) * 32, 32), 32)
        for h in range(2):
            hi, lo = halves(flat[pl.ds(k * 64 + h, 32, stride=2), :])
            uhi[rows, 128 * h : 128 * h + 128] = hi
            ulo[rows, 128 * h : 128 * h + 128] = lo

    arrive(("uc", "low"), ("uc", "high"))
    for k in (0, 1, 2, 3, 13, 14, 15):
        rounded(k)
    arrive(("uy", "up"))
    on_to_core("uc", g, uc_s, uc_r, "up", 2)
    arrive(("uy", "down"))
    on_to_core("uc", g, uc_s, uc_r, "down", 3)
    arrive(("uy", "far"))
    on_to_core("uc", g, uc_s, uc_r, "far", 4)
    arrive(("uc", "up"), ("uc", "down"))
    for k in (4, 5, 6, 10, 11, 12):
        rounded(k)
    arrive(("uc", "far"))
    for k in (7, 8, 9):
        rounded(k)

    mine2 = sz[z]
    arrive("pz")
    for k in range(1, NZ):
        mine2 = mine2 + rz[k]
    two = jnp.concatenate([mine2[j] for j in range(4)], axis=1)
    two_hi = two.astype(BF16).astype(F32)
    stacked = jnp.concatenate([two_hi, two - two_hi, jnp.zeros((12, 512), F32)], axis=0).astype(BF16)
    by_hi = mm(stacked, uhi[...])
    by_lo = mm(stacked, ulo[...])
    two = by_hi[0:2] + (by_hi[2:4] + by_lo[0:2])
    for h in range(2):
        carried = jnp.where(quarter_lane[:2], jnp.where(x // 2 == h, mine2[4], 0.0), 0.0)
        xb[x, 2 * h : 2 * h + 2, :] = carried - two[:, 128 * h : 128 * h + 128]
    for k in (2, 1, 3):
        send("x", xb.at[x], xb.at[x], x_s.at[k], x_r.at[k], to_x[k], xb.at[xp(NX - k)])

    half = quarter // 2

    def partial(k):
        for h in range(2):
            rows = pl.ds(pl.multiple_of(xp(k) * quarter + h * half, half), half)
            left, right = xhi[rows, :], uhi[...]
            prod[k, h] = mm(left, right) + (mm(xlo[rows, :], right) + mm(left, ulo[...]))

    def to_neighbour(name, k, src, at):
        send((name, k), src, xr.at[at], rx_s.at[at], rx_r.at[at], to_x[k], xr.at[at])

    partial(2)
    to_neighbour("relay", 1, prod.at[2, 0], 0)
    to_neighbour("relay", 3, prod.at[2, 1], 1)

    number = jnp.max(jnp.where(quarter_lane[:2], 0.0, mine2[4]), axis=1, keepdims=True)
    left = lax.broadcasted_iota(I32, (1, 128), 1) < 64
    ids[0, y, c] = jnp.where(left, number[0:1], number[1:2])
    for k in FAR_FIRST:
        at = NZ - k
        send("iz", ids.at[0, y, c], ids.at[at, y, c], iz_s.at[k], iz_r.at[k], to_z[k], ids.at[at, y, c])

    arrive("x")
    w[0, y, c] = xb[0] + xb[1] + xb[2] + xb[3]
    def far(k):
        for j in (2, 1, 3, 0):
            send(("wf", j), w.at[0, y, c], w.at[NZ - k, y, c], wz_s.at[k, j], wz_r.at[k, j],
                 dev(zp(k), yp(j), c, x), w.at[NZ - k, yp(NY - j), c])

    def near(k):
        at = NZ - k
        send(("wz", at), w.at[0, y, c], w.at[at, y, c], wz_s.at[k, 0], wz_r.at[k, 0], to_z[k], w.at[at, y, c])

    for step, k in ((far, 8), (far, 7), (far, 9), (near, 5), (near, 11), (far, 6), (far, 10)):
        step(k)
    for k in NEAR:
        near(k)

    partial(1)
    to_neighbour("rx", 1, prod.at[1, 1], 2)
    partial(3)
    to_neighbour("rx", 3, prod.at[3, 0], 3)
    partial(0)

    arrive(*[("wz", at) for at in (1, 2, 3, 4, 5)])
    on_in_y("wy", w, wy_s, wy_r, "w_low", 0)
    arrive(*[("wz", at) for at in (15, 14, 13, 12, 11)])
    on_in_y("wy", w, wy_s, wy_r, "w_high", 1)
    arrive("iz")
    for k in (2, 1, 3):
        send("iy", ids.at[:, y, c], ids.at[:, y, c], iy_s.at[k], iy_r.at[k], to_y[k], ids.at[:, yp(NY - k), c])
    arrive(("relay", 1))
    prod[1, 0] = prod[1, 0] + xr[0]
    to_neighbour("rx2", 1, prod.at[1, 0], 4)
    arrive(("relay", 3))
    prod[3, 1] = prod[3, 1] + xr[1]
    to_neighbour("rx2", 3, prod.at[3, 1], 5)
    arrive(("wy", "w_low"))
    on_to_core("wc", w, wc_s, wc_r, "w_low", 0)
    arrive(("wy", "w_high"))
    on_to_core("wc", w, wc_s, wc_r, "w_high", 1)
    settle(len(sends) - 12)
    arrive(("wf", 0), ("wf", 1), ("wf", 3), ("wf", 2))
    on_to_core("wc", w, wc_s, wc_r, "w_far", 2)
    arrive("iy")
    send("ic", ids.at[:, :, c], ids.at[:, :, c], ic_s.at[0], ic_r.at[0], to_c, ids.at[:, :, 1 - c])
    arrive(("rx", 1), ("rx", 3), ("rx2", 1), ("rx2", 3))
    xs[256 : 256 + half, :] = own[:half, :] - (prod[0, 0] + xr[3] + xr[4])
    xs[256 + half :, :] = own[half:, :] - (prod[0, 1] + xr[2] + xr[5])
    arrive("ic")
    for slot in range(NC * NY * NZ):
        cc, yy, zz = slot // (NY * NZ), slot // NZ % NY, slot % NZ
        rows_ref[slot : slot + 1, :] = ids[(zz - z + NZ) % NZ, yy, cc]

    settle(len(sends) - 4)
    arrive(("wc", "w_low"), ("wc", "w_high"), ("wc", "w_far"))
    for slot in range(NC * NY * NZ):
        cc, yy, zz = slot // (NY * NZ), slot // NZ % NY, slot % NZ
        for h in range(2):
            piece = w[(zz - z + NZ) % NZ, yy, cc, 2 * h : 2 * h + 2, :]
            xs[2 * slot : 2 * slot + 2, 128 * h : 128 * h + 128] = piece

    settle(len(sends))


def factor(xs, dinv, rows_in, first_in, low_ref, up_ref, piv_ref):
    number = rows_in[...].T
    lane = lax.broadcasted_iota(I32, (8, 128), 1)
    for s in range(2):
        even, odd = (
            jnp.take_along_axis(jnp.broadcast_to(number[i : i + 1], (8, 128)), 64 * s + lane // 2, axis=1) for i in (0, 64)
        )
        found = jnp.where(lane % 2 == 0, even, odd)[0:1].astype(I32)
        piv_ref[:, 128 * s : 128 * s + 128] = first_in[:, 128 * s : 128 * s + 128] + found
    right = lax.broadcasted_iota(I32, (64, 128), 1) >= 64
    pivots = [xs[:256, 128 * h : 128 * h + 128] for h in range(2)]
    rest = [xs[256:, 128 * h : 128 * h + 128] for h in range(2)]
    for t in range(4):
        inverse = dinv[t]
        at, first = t // 2, 64 * (t % 2)
        u_t = [v[:64] for v in pivots]
        for h in range(2):
            if h < at:
                shown = jnp.zeros((64, 128), F32)
            else:
                shown = jnp.where(right, u_t[h], 0.0) if h == at and first else u_t[h]
            up_ref[64 * t : 64 * t + 64, 128 * h : 128 * h + 128] = shown
        panel = rest[at][:, first : first + 64]
        low_ref[:, 64 * t : 64 * t + 64] = mm3(panel, inverse)
        if t < 3:
            above = pivots[at][64:, first : first + 64]
            pivots = [v[64:] for v in pivots]
            for h in range(at + (first > 0), 2):
                step = mm3(inverse, jnp.where(right, u_t[h], 0.0) if h == at else u_t[h])
                pivots[h] = pivots[h] - mm3(above, step)
                rest[h] = rest[h] - mm3(panel, step)


def in_hbm(array):
    return pltpu.with_memory_space_constraint(array, pltpu.HBM)


def body(block_column, l_panels, u_blocks, diag_inverses, leaf_pick, merge_pick, final_order):
    rows_dev, cols = block_column.shape
    quarter = rows_dev // NX
    vmem = pl.BlockSpec(memory_space=pltpu.VMEM)
    sem = pltpu.SemaphoreType.DMA
    xs, numbers, first = pl.pallas_call(
        kernel,
        name="panel",
        out_shape=(
            jax.ShapeDtypeStruct((256 + quarter, cols), F32),
            jax.ShapeDtypeStruct((128, 128), F32),
            jax.ShapeDtypeStruct((1, cols), I32),
        ),
        in_specs=[pl.BlockSpec(memory_space=pltpu.HBM)] * 6,
        out_specs=(vmem,) * 3,
        scratch_shapes=[
            pltpu.VMEM((rows_dev * 4 + 8, 128), F32),
            pltpu.VMEM((rows_dev + 8, 128), F32),
            pltpu.VMEM((quarter, cols), F32),
            pltpu.VMEM((1, 256), I32),
            pltpu.VMEM((2, 128, 128), I32),
            pltpu.VMEM((1, 256), I32),
            pltpu.VMEM((4, 256), F32),
            pltpu.VMEM((1, 256), I32),
            pltpu.SMEM((1, 256), I32),
            pltpu.VMEM((rows_dev, 512), BF16),
            pltpu.VMEM((rows_dev, 512), BF16),
            pltpu.VMEM((NZ, NY, NC, 8, 128), F32),
            pltpu.VMEM((NY, 32, 640), F32),
            pltpu.VMEM((NY, 32, 640), F32),
            pltpu.VMEM((NY, 32, 640), F32),
            pltpu.VMEM((NY, 32, 640), F32),
            pltpu.VMEM((32, 640), F32),
            pltpu.VMEM((NZ, 5, 2, 128), F32),
            pltpu.VMEM((NZ, 5, 2, 128), F32),
            pltpu.VMEM((512, cols), BF16),
            pltpu.VMEM((512, cols), BF16),
            pltpu.VMEM((NX, 2, quarter // 2, cols), F32),
            pltpu.VMEM((6, quarter // 2, cols), F32),
            pltpu.VMEM((NX, 4, 128), F32),
            pltpu.VMEM((NZ, NY, NC, 4, 128), F32),
            pltpu.VMEM((NZ, NY, NC, 1, 128), F32),
            sem((9,)),
            pltpu.SemaphoreType.REGULAR,
            sem((NZ,)), sem((NZ,)), sem((4,)), sem((4,)), sem((5, NY)), sem((5, NY)), sem((5,)), sem((5,)),
            sem((NY,)), sem((NY,)), sem((NY,)), sem((NY,)), sem((NZ,)), sem((NZ,)),
            sem((NX,)), sem((NX,)),
            sem((NZ, NY)), sem((NZ, NY)), sem((4, NY)), sem((4, NY)), sem((4,)), sem((4,)),
            sem((6,)), sem((6,)),
            sem((NZ,)), sem((NZ,)), sem((NY,)), sem((NY,)), sem((1,)), sem((1,)),
        ],
        compiler_params=pltpu.CompilerParams(
            collective_id=0, has_side_effects=True, vmem_limit_bytes=24 * 1024 * 1024
        ),
    )(
        in_hbm(l_panels.reshape(-1, 128)),
        in_hbm(block_column),
        in_hbm(u_blocks[0]),
        in_hbm(leaf_pick),
        in_hbm(merge_pick),
        in_hbm(final_order.reshape(1, -1)),
    )
    low, up, piv = pl.pallas_call(
        factor,
        name="factor",
        out_shape=(
            jax.ShapeDtypeStruct((quarter, cols), F32),
            jax.ShapeDtypeStruct((cols, cols), F32),
            jax.ShapeDtypeStruct((1, cols), I32),
        ),
        in_specs=[vmem] * 4,
        out_specs=(vmem,) * 3,
        compiler_params=pltpu.CompilerParams(vmem_limit_bytes=8 * 1024 * 1024),
    )(xs, diag_inverses, numbers, first)
    return low, up, piv[0]


def solution(mesh):
    return jax.shard_map(
        body,
        mesh=mesh,
        in_specs=(
            P("rows", None),
            P("rows", None, "panels", None),
            P("panels", "rows", None),
            P(),
            P("rows", None),
            P(),
            P(),
        ),
        out_specs=(P(("rows", "panels"), None), P(), P()),
        check_vma=False,
    )
```

```python
import functools

import jax
import jax.numpy as jnp
from jax import lax
from jax.experimental import pallas as pl
from jax.experimental.pallas import tpu as pltpu
from jax.sharding import PartitionSpec as P

MESH = pl.DeviceIdType.MESH
F32, BF16, I32 = jnp.float32, jnp.bfloat16, jnp.int32
NZ, NY, NC, NX = 16, 4, 2, 4
FAR_FIRST = (8, 7, 9, 6, 10, 5, 11, 4, 12, 3, 13, 2, 14, 1, 15)
CLOSE = (3, 13, 2, 14, 1, 15)
NEAR = (4, 12) + CLOSE
RANGES = {"low": (0, 4), "high": (13, 16), "up": (4, 7), "down": (10, 13), "far": (7, 10),
          "w_low": (0, 6), "w_high": (11, 16), "w_far": (6, 11)}


SENT = ("uz", "ub", "uy", "uc", "pc", "py", "pz", "x", "wz", "wy", "wc", "rx", "iz", "iy", "ic")
LANDED = (
    "uz", "ub", "ub far", "uy", "uy mid", "uy far", "uc", "uc mid", "uc far", "pc0", "pc1", "pc2", "pc3", "py", "pz", "x",
    "wz low", "wz high", "wz far", "wy low", "wy high", "wc low", "wc high", "wc far", "relay1", "relay3", "rx",
    "iz", "iy", "ic",
)


def halves(v):
    hi = v.astype(BF16)
    return hi, (v - hi.astype(F32)).astype(BF16)


def mm(a, b):
    return jnp.dot(a, b, preferred_element_type=F32)


def mm3(a, b):
    ah, al = halves(a)
    bh, bl = halves(b)
    return mm(jnp.concatenate([ah, al], axis=1), jnp.concatenate([bh, bh], axis=0)) + mm(ah, bl)


def kernel(
    l_hbm, bc_hbm, u_hbm, leaf_hbm, mp_hbm, fo_hbm,
    xs, rows_ref, first_ref,
    l_raw, aux_raw, own, leaf, mp, fo, u_raw, rv, rs,
    xhi, xlo, g, give, keep, rc, ry, b2, sz, rz, uhi, ulo, prod, xr, xb, w, ids,
    in_sem, known, send_sem, recv_sem,
):
    row = lax.axis_index("rows")
    x = lax.axis_index("panels")
    z, y, c = row // (NY * NC), (row // NC) % NY, row % NC
    rows_dev = bc_hbm.shape[0]
    quarter = rows_dev // NX

    def dev(zz, yy, cc, xx):
        return ((zz * NY + yy) * NC + cc, xx)

    def zp(k):
        return (z + k) % NZ

    def yp(k):
        return (y + k) % NY

    def xp(k):
        return (x + k) % NX

    to_z = [dev(zp(k), y, c, x) for k in range(NZ)]
    to_y = [dev(z, yp(k), c, x) for k in range(NY)]
    to_x = [dev(z, y, c, xp(k)) for k in range(NX)]
    to_c = dev(z, y, 1 - c, x)

    col = pl.multiple_of((x // 2) * 128, 128)
    mine = pl.multiple_of(x * quarter, quarter)
    loads = [
        pltpu.make_async_copy(mp_hbm.at[:, pl.ds(0, 128)], mp.at[0], in_sem.at[0]),
        pltpu.make_async_copy(fo_hbm, fo, in_sem.at[1]),
        pltpu.make_async_copy(leaf_hbm, leaf, in_sem.at[2]),
        pltpu.make_async_copy(u_hbm, u_raw, in_sem.at[3]),
        pltpu.make_async_copy(mp_hbm.at[:, pl.ds(128, 128)], mp.at[1], in_sem.at[7]),
        pltpu.make_async_copy(l_hbm, l_raw.at[pl.ds(0, 4 * rows_dev), :], in_sem.at[4]),
        pltpu.make_async_copy(bc_hbm.at[:, pl.ds(col, 128)], aux_raw.at[pl.ds(0, rows_dev), :], in_sem.at[5]),
        pltpu.make_async_copy(bc_hbm.at[pl.ds(mine, quarter), :], own, in_sem.at[6]),
    ]
    barrier = pltpu.get_barrier_semaphore()
    partners = [to_z[k] for k in CLOSE] + to_y[1:] + to_x[1:] + [to_c]
    for partner in partners:
        pl.semaphore_signal(barrier, inc=1, device_id=partner, device_id_type=MESH)

    for copy in loads:
        copy.start()

    l_raw[4 * rows_dev :, :] = jnp.zeros((8, 128), F32)
    aux_raw[rows_dev:, :] = jnp.zeros((8, 128), F32)

    def copy_to(to, src, dst, out, into):
        return pltpu.make_async_remote_copy(
            src, dst, send_sem.at[SENT.index(out)], recv_sem.at[LANDED.index(into)], device_id=to, device_id_type=MESH
        )

    def send(to, src, dst, out, into):
        copy_to(to, src, dst, out, into).start()

    def arrive(into, whole):
        copy_to(to_c, whole, whole, SENT[0], into).wait_recv()

    def sent(out, whole):
        copy_to(to_c, whole, whole, out, LANDED[0]).wait_send()

    for copy in loads[3:4]:
        copy.wait()
    for i in range(4):
        for h in range(2):
            g[0, y, c, 2 * i + h : 2 * i + h + 1, :] = u_raw[i : i + 1, 128 * h : 128 * h + 128]

    for copy in loads[:3] + loads[4:5]:
        copy.wait()
    down = lax.broadcasted_iota(I32, (8, 128), 0)

    def picked(half0, half1, at):
        low = at & 127
        return jnp.where(at >= 128, jnp.take_along_axis(half1, low, axis=1), jnp.take_along_axis(half0, low, axis=1))

    def looked_up(table, first, stride, count, owner, at):
        if count < 8:
            total = jnp.zeros((8, 128), F32)
            for i in range(count):
                line = first + i * stride
                rows = [jnp.broadcast_to(table[h, line : line + 1, :], (8, 128)) for h in range(2)]
                total = jnp.where(owner == i, picked(*rows, at).astype(F32), total)
            return total
        total = jnp.zeros((8, 128), F32)
        for i in range(0, count, 8):
            rows = [table[h, pl.ds(first + i * stride, 8, stride=stride), :] for h in range(2)]
            total += jnp.where(owner - i == down, picked(*rows, at).astype(F32), 0.0)
        return jnp.broadcast_to(jnp.sum(total, axis=0, keepdims=True), (8, 128))

    for s in range(2):
        at = jnp.broadcast_to(fo[:, 128 * s : 128 * s + 128], (8, 128))
        block = jnp.zeros((8, 128), I32)
        for level in reversed(range(7)):
            found = looked_up(mp, 1 << level, 2 << level, 64 >> level, block, at).astype(I32)
            block = 2 * block + (found >> 8)
            at = found & 255
        rows = [jnp.broadcast_to(leaf[:, 128 * h : 128 * h + 128], (8, 128)) for h in range(2)]
        first_ref[:, 128 * s : 128 * s + 128] = rows_dev * block[0:1]
        rv[:, 128 * s : 128 * s + 128] = jnp.where(block == row, picked(*rows, at), rows_dev)[0:1]
    to_scalars = pltpu.make_async_copy(rv, rs, in_sem.at[8])
    to_scalars.start()

    pl.semaphore_wait(barrier, len(partners))
    for k in CLOSE:
        at = NZ - k
        send(to_z[k], g.at[0, y, c], g.at[at, y, c], "uz", "uz")

    to_scalars.wait()
    for copy in loads[5:]:
        copy.wait()

    quarter_lane = lax.broadcasted_iota(I32, (rows_dev, 128), 1) // 64 == x % 2
    numbers = lax.broadcasted_iota(I32, (rows_dev, 128), 0).astype(F32)
    aux_raw[:rows_dev, :] = jnp.where(quarter_lane, aux_raw[:rows_dev, :], numbers)

    def gather(into, core, k):
        base = core * 128 + yp(k) * 32
        for i in range(32):
            at = rs[0, base + i]
            for j in range(4):
                into[i : i + 1, 128 * j : 128 * j + 128] = l_raw[pl.ds(4 * at + j, 1), :]
            into[i : i + 1, 512:640] = aux_raw[pl.ds(at, 1), :]

    def hand_over(k):
        gather(give.at[k], 1 - c, k)
        send(to_c, give.at[k], rc.at[k], "pc", f"pc{k}")

    def fold(k):
        gather(keep.at[k], c, k)
        arrive(f"pc{k}", rc.at[k])
        keep[k] = keep[k] + rc[k]
        send(to_y[k], keep.at[k], ry.at[k], "py", "py")

    hand_over(2)
    hand_over(1)
    fold(2)
    hand_over(3)
    fold(1)
    hand_over(0)
    fold(3)
    gather(keep.at[0], c, 0)
    arrive("pc0", rc.at[0])

    def on_in_y(buf, which, out, into):
        first, last = RANGES[which]
        part = pl.ds(first, last - first)
        for k in (2, 1, 3):
            send(to_y[k], buf.at[part, y, c], buf.at[part, y, c], out, into)

    def on_to_core(buf, which, out, into):
        first, last = RANGES[which]
        part = pl.ds(first, last - first)
        send(to_c, buf.at[part, :, c], buf.at[part, :, c], out, into)

    def second(into, k, first, last, there):
        src, dst = pl.ds(first, last - first), pl.ds(there, last - first)
        send(to_z[k], g.at[src, y, c], g.at[dst, y, c], "ub", into)

    arrive("uz", g.at[pl.ds(0, 6), y, c])
    second("ub far", 11, 2, 4, 7)
    second("ub far", 5, 14, 15, 9)
    second("ub", 13, 1, 4, 4)
    second("ub", 3, 13, 16, 10)
    for k in (3, 13):
        pl.semaphore_signal(known, inc=1, device_id=to_z[k], device_id_type=MESH)

    for part in range(NX):
        rows = pl.ds(part * quarter, quarter)
        for j in range(4):
            hi, lo = halves(l_raw[pl.ds(part * quarter * 4 + j, quarter, stride=4), :])
            xhi[rows, 128 * j : 128 * j + 128] = hi
            xlo[rows, 128 * j : 128 * j + 128] = lo

    arrive("py", ry.at[pl.ds(1, 3)])
    b2[...] = keep[0] + rc[0] + ry[1] + ry[2] + ry[3]
    for zz in range(NZ):
        for j in range(5):
            sz[zz, j] = b2[2 * zz : 2 * zz + 2, 128 * j : 128 * j + 128]
    pl.semaphore_wait(known, 2)
    for k in FAR_FIRST:
        send(to_z[k], sz.at[zp(k)], rz.at[k], "pz", "pz")
    on_in_y(g, "low", "uy", "uy")
    on_in_y(g, "high", "uy", "uy")
    arrive("ub", g.at[pl.ds(0, 6), y, c])
    on_in_y(g, "up", "uy", "uy mid")
    on_in_y(g, "down", "uy", "uy mid")
    arrive("ub far", g.at[pl.ds(0, 3), y, c])
    on_in_y(g, "far", "uy", "uy far")
    arrive("uy", g.at[pl.ds(0, 7), pl.ds(0, 3), c])
    on_to_core(g, "low", "uc", "uc")
    on_to_core(g, "high", "uc", "uc")
    flat = g.reshape(NZ * NY * NC * 8, 128)

    def rounded(k):
        rows = pl.ds(pl.multiple_of(zp(k) * 32, 32), 32)
        for h in range(2):
            hi, lo = halves(flat[pl.ds(k * 64 + h, 32, stride=2), :])
            uhi[rows, 128 * h : 128 * h + 128] = hi
            ulo[rows, 128 * h : 128 * h + 128] = lo

    arrive("uc", g.at[pl.ds(0, 7), :, c])
    for k in (0, 1, 2, 3, 13, 14, 15):
        rounded(k)
    arrive("uy mid", g.at[pl.ds(0, 6), pl.ds(0, 3), c])
    on_to_core(g, "up", "uc", "uc mid")
    on_to_core(g, "down", "uc", "uc mid")
    arrive("uy far", g.at[pl.ds(0, 3), pl.ds(0, 3), c])
    on_to_core(g, "far", "uc", "uc far")
    arrive("uc mid", g.at[pl.ds(0, 6), :, c])
    for k in (4, 5, 6, 10, 11, 12):
        rounded(k)
    arrive("uc far", g.at[pl.ds(0, 3), :, c])
    for k in (7, 8, 9):
        rounded(k)

    mine2 = sz[z]
    arrive("pz", rz.at[pl.ds(1, NZ - 1)])
    for k in range(1, NZ):
        mine2 = mine2 + rz[k]
    two = jnp.concatenate([mine2[j] for j in range(4)], axis=1)
    two_hi = two.astype(BF16).astype(F32)
    stacked = jnp.concatenate([two_hi, two - two_hi, jnp.zeros((12, 512), F32)], axis=0).astype(BF16)
    by_hi = mm(stacked, uhi[...])
    by_lo = mm(stacked, ulo[...])
    two = by_hi[0:2] + (by_hi[2:4] + by_lo[0:2])
    for h in range(2):
        carried = jnp.where(quarter_lane[:2], jnp.where(x // 2 == h, mine2[4], 0.0), 0.0)
        xb[x, 2 * h : 2 * h + 2, :] = carried - two[:, 128 * h : 128 * h + 128]
    for k in (2, 1, 3):
        send(to_x[k], xb.at[x], xb.at[x], "x", "x")

    half = quarter // 2

    def partial(k):
        for h in range(2):
            rows = pl.ds(pl.multiple_of(xp(k) * quarter + h * half, half), half)
            left, right = xhi[rows, :], uhi[...]
            prod[k, h] = mm(left, right) + (mm(xlo[rows, :], right) + mm(left, ulo[...]))

    def to_neighbour(into, k, src, at):
        send(to_x[k], src, xr.at[at], "rx", into)

    partial(2)
    to_neighbour("relay1", 1, prod.at[2, 0], 0)
    to_neighbour("relay3", 3, prod.at[2, 1], 1)

    number = jnp.max(jnp.where(quarter_lane[:2], 0.0, mine2[4]), axis=1, keepdims=True)
    left = lax.broadcasted_iota(I32, (1, 128), 1) < 64
    ids[0, y, c] = jnp.where(left, number[0:1], number[1:2])
    for k in FAR_FIRST:
        at = NZ - k
        send(to_z[k], ids.at[0, y, c], ids.at[at, y, c], "iz", "iz")

    arrive("x", xb.at[pl.ds(0, 3)])
    w[0, y, c] = xb[0] + xb[1] + xb[2] + xb[3]
    def far(k):
        for j in (2, 1, 3, 0):
            send(dev(zp(k), yp(j), c, x), w.at[0, y, c], w.at[NZ - k, y, c], "wz", "wz far")

    def near(k):
        send(to_z[k], w.at[0, y, c], w.at[NZ - k, y, c], "wz", "wz low" if NZ - k < 8 else "wz high")

    for step, k in ((far, 8), (far, 7), (far, 9), (near, 5), (near, 11), (far, 6), (far, 10)):
        step(k)
    for k in NEAR:
        near(k)

    partial(1)
    to_neighbour("rx", 1, prod.at[1, 1], 2)
    partial(3)
    to_neighbour("rx", 3, prod.at[3, 0], 3)
    partial(0)

    arrive("wz low", w.at[pl.ds(0, 5), y, c])
    on_in_y(w, "w_low", "wy", "wy low")
    arrive("wz high", w.at[pl.ds(0, 5), y, c])
    on_in_y(w, "w_high", "wy", "wy high")
    arrive("iz", ids.at[pl.ds(1, NZ - 1), y, c])
    for k in (2, 1, 3):
        send(to_y[k], ids.at[:, y, c], ids.at[:, y, c], "iy", "iy")
    arrive("relay1", xr.at[0])
    prod[1, 0] = prod[1, 0] + xr[0]
    to_neighbour("rx", 1, prod.at[1, 0], 4)
    arrive("relay3", xr.at[1])
    prod[3, 1] = prod[3, 1] + xr[1]
    to_neighbour("rx", 3, prod.at[3, 1], 5)
    arrive("wy low", w.at[pl.ds(0, 6), pl.ds(0, 3), c])
    on_to_core(w, "w_low", "wc", "wc low")
    arrive("wy high", w.at[pl.ds(0, 5), pl.ds(0, 3), c])
    on_to_core(w, "w_high", "wc", "wc high")
    sent("uz", g.at[pl.ds(0, 6), y, c])
    sent("ub", g.at[pl.ds(0, 9), y, c])
    sent("uy", g.at[:, pl.ds(0, 3), c])
    sent("uc", g.at[:, :, c])
    sent("pc", give)
    sent("py", keep.at[pl.ds(0, 3)])
    sent("pz", sz.at[pl.ds(0, NZ - 1)])
    sent("x", xb.at[pl.ds(0, 3)])
    sent("iz", ids.at[pl.ds(0, NZ - 1), y, c])
    arrive("wz far", w.at[pl.ds(0, 5), :, c])
    on_to_core(w, "w_far", "wc", "wc far")
    arrive("iy", ids.at[:, pl.ds(0, 3), c])
    send(to_c, ids.at[:, :, c], ids.at[:, :, c], "ic", "ic")
    arrive("rx", xr.at[pl.ds(2, 4)])
    xs[256 : 256 + half, :] = own[:half, :] - (prod[0, 0] + xr[3] + xr[4])
    xs[256 + half :, :] = own[half:, :] - (prod[0, 1] + xr[2] + xr[5])
    arrive("ic", ids.at[:, :, 1 - c])
    for slot in range(NC * NY * NZ):
        cc, yy, zz = slot // (NY * NZ), slot // NZ % NY, slot % NZ
        rows_ref[slot : slot + 1, :] = ids[(zz - z + NZ) % NZ, yy, cc]

    sent("wz", w.at[pl.ds(0, 15), pl.ds(0, 2), c])
    sent("wy", w.at[pl.ds(0, 11), pl.ds(0, 3), c])
    sent("rx", xr)
    sent("iy", ids.at[:, pl.ds(0, 3), c])
    arrive("wc low", w.at[pl.ds(0, 6), :, c])
    arrive("wc high", w.at[pl.ds(0, 5), :, c])
    arrive("wc far", w.at[pl.ds(0, 5), :, c])
    for slot in range(NC * NY * NZ):
        cc, yy, zz = slot // (NY * NZ), slot // NZ % NY, slot % NZ
        for h in range(2):
            piece = w[(zz - z + NZ) % NZ, yy, cc, 2 * h : 2 * h + 2, :]
            xs[2 * slot : 2 * slot + 2, 128 * h : 128 * h + 128] = piece

    sent("wc", w.at[:, :, c])
    sent("ic", ids.at[:, :, c])


def factor(xs, dinv, rows_in, first_in, low_ref, up_ref, piv_ref):
    number = rows_in[...].T
    lane = lax.broadcasted_iota(I32, (8, 128), 1)
    for s in range(2):
        even, odd = (
            jnp.take_along_axis(jnp.broadcast_to(number[i : i + 1], (8, 128)), 64 * s + lane // 2, axis=1) for i in (0, 64)
        )
        found = jnp.where(lane % 2 == 0, even, odd)[0:1].astype(I32)
        piv_ref[:, 128 * s : 128 * s + 128] = first_in[:, 128 * s : 128 * s + 128] + found
    right = lax.broadcasted_iota(I32, (64, 128), 1) >= 64
    pivots = [xs[:256, 128 * h : 128 * h + 128] for h in range(2)]
    rest = [xs[256:, 128 * h : 128 * h + 128] for h in range(2)]
    for t in range(4):
        inverse = dinv[t]
        at, first = t // 2, 64 * (t % 2)
        u_t = [v[:64] for v in pivots]
        for h in range(2):
            if h < at:
                shown = jnp.zeros((64, 128), F32)
            else:
                shown = jnp.where(right, u_t[h], 0.0) if h == at and first else u_t[h]
            up_ref[64 * t : 64 * t + 64, 128 * h : 128 * h + 128] = shown
        panel = rest[at][:, first : first + 64]
        low_ref[:, 64 * t : 64 * t + 64] = mm3(panel, inverse)
        if t < 3:
            above = pivots[at][64:, first : first + 64]
            pivots = [v[64:] for v in pivots]
            for h in range(at + (first > 0), 2):
                step = mm3(inverse, jnp.where(right, u_t[h], 0.0) if h == at else u_t[h])
                pivots[h] = pivots[h] - mm3(above, step)
                rest[h] = rest[h] - mm3(panel, step)


def in_hbm(array):
    return pltpu.with_memory_space_constraint(array, pltpu.HBM)


def body(block_column, l_panels, u_blocks, diag_inverses, leaf_pick, merge_pick, final_order):
    rows_dev, cols = block_column.shape
    quarter = rows_dev // NX
    vmem = pl.BlockSpec(memory_space=pltpu.VMEM)
    sem = pltpu.SemaphoreType.DMA
    xs, numbers, first = pl.pallas_call(
        kernel,
        name="panel",
        out_shape=(
            jax.ShapeDtypeStruct((256 + quarter, cols), F32),
            jax.ShapeDtypeStruct((128, 128), F32),
            jax.ShapeDtypeStruct((1, cols), I32),
        ),
        in_specs=[pl.BlockSpec(memory_space=pltpu.HBM)] * 6,
        out_specs=(vmem,) * 3,
        scratch_shapes=[
            pltpu.VMEM((rows_dev * 4 + 8, 128), F32),
            pltpu.VMEM((rows_dev + 8, 128), F32),
            pltpu.VMEM((quarter, cols), F32),
            pltpu.VMEM((1, 256), I32),
            pltpu.VMEM((2, 128, 128), I32),
            pltpu.VMEM((1, 256), I32),
            pltpu.VMEM((4, 256), F32),
            pltpu.VMEM((1, 256), I32),
            pltpu.SMEM((1, 256), I32),
            pltpu.VMEM((rows_dev, 512), BF16),
            pltpu.VMEM((rows_dev, 512), BF16),
            pltpu.VMEM((NZ, NY, NC, 8, 128), F32),
            pltpu.VMEM((NY, 32, 640), F32),
            pltpu.VMEM((NY, 32, 640), F32),
            pltpu.VMEM((NY, 32, 640), F32),
            pltpu.VMEM((NY, 32, 640), F32),
            pltpu.VMEM((32, 640), F32),
            pltpu.VMEM((NZ, 5, 2, 128), F32),
            pltpu.VMEM((NZ, 5, 2, 128), F32),
            pltpu.VMEM((512, cols), BF16),
            pltpu.VMEM((512, cols), BF16),
            pltpu.VMEM((NX, 2, quarter // 2, cols), F32),
            pltpu.VMEM((6, quarter // 2, cols), F32),
            pltpu.VMEM((NX, 4, 128), F32),
            pltpu.VMEM((NZ, NY, NC, 4, 128), F32),
            pltpu.VMEM((NZ, NY, NC, 1, 128), F32),
            sem((9,)),
            pltpu.SemaphoreType.REGULAR,
            sem((len(SENT),)),
            sem((len(LANDED),)),
        ],
        compiler_params=pltpu.CompilerParams(
            collective_id=0, has_side_effects=True, vmem_limit_bytes=24 * 1024 * 1024
        ),
    )(
        in_hbm(l_panels.reshape(-1, 128)),
        in_hbm(block_column),
        in_hbm(u_blocks[0]),
        in_hbm(leaf_pick),
        in_hbm(merge_pick),
        in_hbm(final_order.reshape(1, -1)),
    )
    low, up, piv = pl.pallas_call(
        factor,
        name="factor",
        out_shape=(
            jax.ShapeDtypeStruct((quarter, cols), F32),
            jax.ShapeDtypeStruct((cols, cols), F32),
            jax.ShapeDtypeStruct((1, cols), I32),
        ),
        in_specs=[vmem] * 4,
        out_specs=(vmem,) * 3,
        compiler_params=pltpu.CompilerParams(vmem_limit_bytes=8 * 1024 * 1024),
    )(xs, diag_inverses, numbers, first)
    return low, up, piv[0]


def solution(mesh):
    return jax.shard_map(
        body,
        mesh=mesh,
        in_specs=(
            P("rows", None),
            P("rows", None, "panels", None),
            P("panels", "rows", None),
            P(),
            P("rows", None),
            P(),
            P(),
        ),
        out_specs=(P(("rows", "panels"), None), P(), P()),
        check_vma=False,
    )
```

```python
import functools

import jax
import jax.numpy as jnp
from jax import lax
from jax.experimental import pallas as pl
from jax.experimental.pallas import tpu as pltpu
from jax.sharding import PartitionSpec as P

MESH = pl.DeviceIdType.MESH
F32, BF16, I32 = jnp.float32, jnp.bfloat16, jnp.int32
NZ, NY, NC, NX = 16, 4, 2, 4
FAR_FIRST = (8, 7, 9, 6, 10, 5, 11, 4, 12, 3, 13, 2, 14, 1, 15)
CLOSE = (3, 13, 2, 14, 1, 15)
NEAR = (4, 12) + CLOSE
RANGES = {"low": (0, 4), "high": (13, 16), "up": (4, 7), "down": (10, 13), "far": (7, 10),
          "w_low": (0, 6), "w_high": (11, 16), "w_far": (6, 11)}


SENT = ("uz", "ub", "uy", "uc", "pc", "py", "pz", "x", "wz", "wy", "wc", "rx", "nc", "ny", "nz")
LANDED = (
    "uz", "ub", "ub far", "uy", "uy mid", "uy far", "uc", "uc mid", "uc far", "pc0", "pc1", "pc2", "pc3", "py", "pz", "x",
    "wz low", "wz high", "wz far", "wy low", "wy high", "wc low", "wc high", "wc far", "relay1", "relay3", "rx",
    "nc", "ny", "nz",
)


def halves(v):
    hi = v.astype(BF16)
    return hi, (v - hi.astype(F32)).astype(BF16)


def mm(a, b):
    return jnp.dot(a, b, preferred_element_type=F32)


def mm3(a, b):
    ah, al = halves(a)
    bh, bl = halves(b)
    return mm(jnp.concatenate([ah, al], axis=1), jnp.concatenate([bh, bh], axis=0)) + mm(ah, bl)


def kernel(
    l_hbm, bc_hbm, u_hbm, leaf_hbm, mp_hbm, fo_hbm,
    xs, piv_ref,
    l_raw, aux_raw, own, leaf, mp, fo, u_raw, rv, rs,
    xhi, xlo, g, give, keep, rc, ry, b2, sz, rz, uhi, ulo, prod, xr, xb, w, nv, nc, ny, nz,
    in_sem, known, send_sem, recv_sem,
):
    row = lax.axis_index("rows")
    x = lax.axis_index("panels")
    z, y, c = row // (NY * NC), (row // NC) % NY, row % NC
    rows_dev = bc_hbm.shape[0]
    quarter = rows_dev // NX

    def dev(zz, yy, cc, xx):
        return ((zz * NY + yy) * NC + cc, xx)

    def zp(k):
        return (z + k) % NZ

    def yp(k):
        return (y + k) % NY

    def xp(k):
        return (x + k) % NX

    to_z = [dev(zp(k), y, c, x) for k in range(NZ)]
    to_y = [dev(z, yp(k), c, x) for k in range(NY)]
    to_x = [dev(z, y, c, xp(k)) for k in range(NX)]
    to_c = dev(z, y, 1 - c, x)

    col = pl.multiple_of((x // 2) * 128, 128)
    mine = pl.multiple_of(x * quarter, quarter)
    loads = [
        pltpu.make_async_copy(mp_hbm.at[:, pl.ds(0, 128)], mp.at[0], in_sem.at[0]),
        pltpu.make_async_copy(fo_hbm, fo, in_sem.at[1]),
        pltpu.make_async_copy(leaf_hbm, leaf, in_sem.at[2]),
        pltpu.make_async_copy(u_hbm, u_raw, in_sem.at[3]),
        pltpu.make_async_copy(mp_hbm.at[:, pl.ds(128, 128)], mp.at[1], in_sem.at[7]),
        pltpu.make_async_copy(l_hbm, l_raw.at[pl.ds(0, 4 * rows_dev), :], in_sem.at[4]),
        pltpu.make_async_copy(bc_hbm.at[:, pl.ds(col, 128)], aux_raw.at[pl.ds(0, rows_dev), :], in_sem.at[5]),
        pltpu.make_async_copy(bc_hbm.at[pl.ds(mine, quarter), :], own, in_sem.at[6]),
    ]
    barrier = pltpu.get_barrier_semaphore()
    partners = [to_z[k] for k in CLOSE] + to_y[1:] + to_x[1:] + [to_c]
    for partner in partners:
        pl.semaphore_signal(barrier, inc=1, device_id=partner, device_id_type=MESH)

    for copy in loads:
        copy.start()

    l_raw[4 * rows_dev :, :] = jnp.zeros((8, 128), F32)
    aux_raw[rows_dev:, :] = jnp.zeros((8, 128), F32)

    def copy_to(to, src, dst, out, into):
        return pltpu.make_async_remote_copy(
            src, dst, send_sem.at[SENT.index(out)], recv_sem.at[LANDED.index(into)], device_id=to, device_id_type=MESH
        )

    def send(to, src, dst, out, into):
        copy_to(to, src, dst, out, into).start()

    def arrive(into, whole):
        copy_to(to_c, whole, whole, SENT[0], into).wait_recv()

    def sent(out, whole):
        copy_to(to_c, whole, whole, out, LANDED[0]).wait_send()

    for copy in loads[3:4]:
        copy.wait()
    for i in range(4):
        for h in range(2):
            g[0, y, c, 2 * i + h : 2 * i + h + 1, :] = u_raw[i : i + 1, 128 * h : 128 * h + 128]

    for copy in loads[:3] + loads[4:5]:
        copy.wait()
    down = lax.broadcasted_iota(I32, (8, 128), 0)

    def picked(half0, half1, at):
        low = at & 127
        return jnp.where(at >= 128, jnp.take_along_axis(half1, low, axis=1), jnp.take_along_axis(half0, low, axis=1))

    def looked_up(table, first, stride, count, owner, at):
        if count < 8:
            total = jnp.zeros((8, 128), F32)
            for i in range(count):
                line = first + i * stride
                rows = [jnp.broadcast_to(table[h, line : line + 1, :], (8, 128)) for h in range(2)]
                total = jnp.where(owner == i, picked(*rows, at).astype(F32), total)
            return total
        total = jnp.zeros((8, 128), F32)
        for i in range(0, count, 8):
            rows = [table[h, pl.ds(first + i * stride, 8, stride=stride), :] for h in range(2)]
            total += jnp.where(owner - i == down, picked(*rows, at).astype(F32), 0.0)
        return jnp.broadcast_to(jnp.sum(total, axis=0, keepdims=True), (8, 128))

    for s in range(2):
        at = jnp.broadcast_to(fo[:, 128 * s : 128 * s + 128], (8, 128))
        block = jnp.zeros((8, 128), I32)
        for level in reversed(range(7)):
            found = looked_up(mp, 1 << level, 2 << level, 64 >> level, block, at).astype(I32)
            block = 2 * block + (found >> 8)
            at = found & 255
        rows = [jnp.broadcast_to(leaf[:, 128 * h : 128 * h + 128], (8, 128)) for h in range(2)]
        line = picked(*rows, at)
        rv[:, 128 * s : 128 * s + 128] = jnp.where(block == row, line, rows_dev)[0:1]
        nv[:, 128 * s : 128 * s + 128] = jnp.where(block == row, rows_dev * block + line, 0)[0:1]
    to_scalars = pltpu.make_async_copy(rv, rs, in_sem.at[8])
    to_scalars.start()

    pl.semaphore_wait(barrier, len(partners))
    for k in CLOSE:
        at = NZ - k
        send(to_z[k], g.at[0, y, c], g.at[at, y, c], "uz", "uz")

    to_scalars.wait()
    for copy in loads[5:]:
        copy.wait()

    quarter_lane = lax.broadcasted_iota(I32, (rows_dev, 128), 1) // 64 == x % 2
    wide = aux_raw[:rows_dev, :]
    aux_raw[:rows_dev, :] = jnp.where(quarter_lane, wide, pltpu.roll(wide, 64, axis=1))
    left = lax.broadcasted_iota(I32, (8, 128), 1) < 64

    def gather(into, core, k):
        base = core * 128 + yp(k) * 32
        for i in range(0, 32, 2):
            pair = rs[0, base + i], rs[0, base + i + 1]
            for n in range(8):
                into[4 * i + n : 4 * i + n + 1, :] = l_raw[pl.ds(4 * pair[n // 4] + n % 4, 1), :]
            first, second = (aux_raw[pl.ds(at, 1), :] for at in pair)
            into[128 + i // 2 : 129 + i // 2, :] = jnp.where(left[:1], first, second)

    def hand_over(k):
        gather(give.at[k], 1 - c, k)
        send(to_c, give.at[k], rc.at[k], "pc", f"pc{k}")

    def fold(k):
        gather(keep.at[k], c, k)
        arrive(f"pc{k}", rc.at[k])
        keep[k] = keep[k] + rc[k]
        send(to_y[k], keep.at[k], ry.at[k], "py", "py")

    send(to_c, nv, nc, "nc", "nc")
    hand_over(2)
    hand_over(1)
    fold(2)
    hand_over(3)
    fold(1)
    hand_over(0)
    fold(3)
    gather(keep.at[0], c, 0)
    arrive("pc0", rc.at[0])
    arrive("nc", nc)
    ny[0] = nv[...] + nc[...]
    for k in (2, 1, 3):
        send(to_y[k], ny.at[0], ny.at[k], "ny", "ny")

    def on_in_y(buf, which, out, into):
        first, last = RANGES[which]
        part = pl.ds(first, last - first)
        for k in (2, 1, 3):
            send(to_y[k], buf.at[part, y, c], buf.at[part, y, c], out, into)

    def on_to_core(buf, which, out, into):
        first, last = RANGES[which]
        part = pl.ds(first, last - first)
        send(to_c, buf.at[part, :, c], buf.at[part, :, c], out, into)

    def second(into, k, first, last, there):
        src, dst = pl.ds(first, last - first), pl.ds(there, last - first)
        send(to_z[k], g.at[src, y, c], g.at[dst, y, c], "ub", into)

    arrive("uz", g.at[pl.ds(0, 6), y, c])
    second("ub far", 11, 2, 4, 7)
    second("ub far", 5, 14, 15, 9)
    second("ub", 13, 1, 4, 4)
    second("ub", 3, 13, 16, 10)
    for k in (3, 13):
        pl.semaphore_signal(known, inc=1, device_id=to_z[k], device_id_type=MESH)

    for part in range(NX):
        rows = pl.ds(part * quarter, quarter)
        for j in range(4):
            hi, lo = halves(l_raw[pl.ds(part * quarter * 4 + j, quarter, stride=4), :])
            xhi[rows, 128 * j : 128 * j + 128] = hi
            xlo[rows, 128 * j : 128 * j + 128] = lo

    arrive("py", ry.at[pl.ds(1, 3)])
    b2[...] = keep[0] + rc[0] + ry[1] + ry[2] + ry[3]
    for zz in range(NZ):
        for line in range(9):
            at = 8 * zz + line if line < 8 else 128 + zz
            sz[zz, line] = b2[at : at + 1, :]
    pl.semaphore_wait(known, 2)
    for k in FAR_FIRST:
        send(to_z[k], sz.at[zp(k)], rz.at[k], "pz", "pz")
    on_in_y(g, "low", "uy", "uy")
    on_in_y(g, "high", "uy", "uy")
    arrive("ub", g.at[pl.ds(0, 6), y, c])
    on_in_y(g, "up", "uy", "uy mid")
    on_in_y(g, "down", "uy", "uy mid")
    arrive("ub far", g.at[pl.ds(0, 3), y, c])
    on_in_y(g, "far", "uy", "uy far")
    arrive("uy", g.at[pl.ds(0, 7), pl.ds(0, 3), c])
    on_to_core(g, "low", "uc", "uc")
    on_to_core(g, "high", "uc", "uc")
    flat = g.reshape(NZ * NY * NC * 8, 128)

    def rounded(k):
        rows = pl.ds(pl.multiple_of(zp(k) * 32, 32), 32)
        for h in range(2):
            hi, lo = halves(flat[pl.ds(k * 64 + h, 32, stride=2), :])
            uhi[rows, 128 * h : 128 * h + 128] = hi
            ulo[rows, 128 * h : 128 * h + 128] = lo

    arrive("uc", g.at[pl.ds(0, 7), :, c])
    for k in (0, 1, 2, 3, 13, 14, 15):
        rounded(k)
    arrive("uy mid", g.at[pl.ds(0, 6), pl.ds(0, 3), c])
    on_to_core(g, "up", "uc", "uc mid")
    on_to_core(g, "down", "uc", "uc mid")
    arrive("uy far", g.at[pl.ds(0, 3), pl.ds(0, 3), c])
    on_to_core(g, "far", "uc", "uc far")
    arrive("uc mid", g.at[pl.ds(0, 6), :, c])
    for k in (4, 5, 6, 10, 11, 12):
        rounded(k)
    arrive("uc far", g.at[pl.ds(0, 3), :, c])
    for k in (7, 8, 9):
        rounded(k)

    mine2 = sz[z]
    arrive("pz", rz.at[pl.ds(1, NZ - 1)])
    for k in range(1, NZ):
        mine2 = mine2 + rz[k]
    two = jnp.concatenate([jnp.concatenate([mine2[4 * i + j] for j in range(4)], axis=1) for i in range(2)], axis=0)
    two_hi = two.astype(BF16).astype(F32)
    stacked = jnp.concatenate([two_hi, two - two_hi, jnp.zeros((12, 512), F32)], axis=0).astype(BF16)
    by_hi = mm(stacked, uhi[...])
    by_lo = mm(stacked, ulo[...])
    two = by_hi[0:2] + (by_hi[2:4] + by_lo[0:2])
    both = jnp.broadcast_to(mine2[8], (8, 128))
    swapped = pltpu.roll(both, 64, axis=1)
    both = jnp.concatenate([jnp.where(left, both, swapped)[:1], jnp.where(left, swapped, both)[:1]], axis=0)
    for h in range(2):
        carried = jnp.where(quarter_lane[:2], jnp.where(x // 2 == h, both, 0.0), 0.0)
        xb[x, 2 * h : 2 * h + 2, :] = carried - two[:, 128 * h : 128 * h + 128]
    for k in (2, 1, 3):
        send(to_x[k], xb.at[x], xb.at[x], "x", "x")

    half = quarter // 2

    def partial(k):
        for h in range(2):
            rows = pl.ds(pl.multiple_of(xp(k) * quarter + h * half, half), half)
            left, right = xhi[rows, :], uhi[...]
            prod[k, h] = mm(left, right) + (mm(xlo[rows, :], right) + mm(left, ulo[...]))

    def to_neighbour(into, k, src, at):
        send(to_x[k], src, xr.at[at], "rx", into)

    partial(2)
    to_neighbour("relay1", 1, prod.at[2, 0], 0)
    to_neighbour("relay3", 3, prod.at[2, 1], 1)

    arrive("ny", ny.at[pl.ds(1, 3)])
    nz[0] = ny[0] + ny[1] + ny[2] + ny[3]
    for k in FAR_FIRST:
        send(to_z[k], nz.at[0], nz.at[k], "nz", "nz")

    arrive("x", xb.at[pl.ds(0, 3)])
    w[0, y, c] = xb[0] + xb[1] + xb[2] + xb[3]
    def far(k):
        for j in (2, 1, 3, 0):
            send(dev(zp(k), yp(j), c, x), w.at[0, y, c], w.at[NZ - k, y, c], "wz", "wz far")

    def near(k):
        send(to_z[k], w.at[0, y, c], w.at[NZ - k, y, c], "wz", "wz low" if NZ - k < 8 else "wz high")

    for step, k in ((far, 8), (far, 7), (far, 9), (near, 5), (near, 11), (far, 6), (far, 10)):
        step(k)
    for k in NEAR:
        near(k)

    partial(1)
    to_neighbour("rx", 1, prod.at[1, 1], 2)
    partial(3)
    to_neighbour("rx", 3, prod.at[3, 0], 3)
    partial(0)

    arrive("wz low", w.at[pl.ds(0, 5), y, c])
    on_in_y(w, "w_low", "wy", "wy low")
    arrive("wz high", w.at[pl.ds(0, 5), y, c])
    on_in_y(w, "w_high", "wy", "wy high")
    arrive("relay1", xr.at[0])
    prod[1, 0] = prod[1, 0] + xr[0]
    to_neighbour("rx", 1, prod.at[1, 0], 4)
    arrive("relay3", xr.at[1])
    prod[3, 1] = prod[3, 1] + xr[1]
    to_neighbour("rx", 3, prod.at[3, 1], 5)
    arrive("wy low", w.at[pl.ds(0, 6), pl.ds(0, 3), c])
    on_to_core(w, "w_low", "wc", "wc low")
    arrive("wy high", w.at[pl.ds(0, 5), pl.ds(0, 3), c])
    on_to_core(w, "w_high", "wc", "wc high")
    sent("uz", g.at[pl.ds(0, 6), y, c])
    sent("ub", g.at[pl.ds(0, 9), y, c])
    sent("uy", g.at[:, pl.ds(0, 3), c])
    sent("uc", g.at[:, :, c])
    sent("pc", give)
    sent("py", keep.at[pl.ds(0, 3)])
    sent("pz", sz.at[pl.ds(0, NZ - 1)])
    sent("x", xb.at[pl.ds(0, 3)])
    sent("nc", nv)
    sent("ny", ny.at[pl.ds(1, 3)])
    sent("nz", nz.at[pl.ds(1, NZ - 1)])
    arrive("wz far", w.at[pl.ds(0, 5), :, c])
    on_to_core(w, "w_far", "wc", "wc far")
    arrive("rx", xr.at[pl.ds(2, 4)])
    xs[256 : 256 + half, :] = own[:half, :] - (prod[0, 0] + xr[3] + xr[4])
    xs[256 + half :, :] = own[half:, :] - (prod[0, 1] + xr[2] + xr[5])
    arrive("nz", nz.at[pl.ds(1, NZ - 1)])
    number = nz[0]
    for k in range(1, NZ):
        number = number + nz[k]
    piv_ref[...] = number
    sent("wz", w.at[pl.ds(0, 15), pl.ds(0, 2), c])
    sent("wy", w.at[pl.ds(0, 11), pl.ds(0, 3), c])
    sent("rx", xr)
    arrive("wc low", w.at[pl.ds(0, 6), :, c])
    arrive("wc high", w.at[pl.ds(0, 5), :, c])
    arrive("wc far", w.at[pl.ds(0, 5), :, c])
    for slot in range(NC * NY * NZ):
        cc, yy, zz = slot // (NY * NZ), slot // NZ % NY, slot % NZ
        for h in range(2):
            piece = w[(zz - z + NZ) % NZ, yy, cc, 2 * h : 2 * h + 2, :]
            xs[2 * slot : 2 * slot + 2, 128 * h : 128 * h + 128] = piece

    sent("wc", w.at[:, :, c])


def factor(xs, dinv, piv_in, low_ref, up_ref, piv_ref):
    piv_ref[...] = piv_in[...]
    right = lax.broadcasted_iota(I32, (64, 128), 1) >= 64
    pivots = [xs[:256, 128 * h : 128 * h + 128] for h in range(2)]
    rest = [xs[256:, 128 * h : 128 * h + 128] for h in range(2)]
    for t in range(4):
        inverse = dinv[t]
        at, first = t // 2, 64 * (t % 2)
        u_t = [v[:64] for v in pivots]
        for h in range(2):
            if h < at:
                shown = jnp.zeros((64, 128), F32)
            else:
                shown = jnp.where(right, u_t[h], 0.0) if h == at and first else u_t[h]
            up_ref[64 * t : 64 * t + 64, 128 * h : 128 * h + 128] = shown
        panel = rest[at][:, first : first + 64]
        low_ref[:, 64 * t : 64 * t + 64] = mm3(panel, inverse)
        if t < 3:
            above = pivots[at][64:, first : first + 64]
            pivots = [v[64:] for v in pivots]
            for h in range(at + (first > 0), 2):
                step = mm3(inverse, jnp.where(right, u_t[h], 0.0) if h == at else u_t[h])
                pivots[h] = pivots[h] - mm3(above, step)
                rest[h] = rest[h] - mm3(panel, step)


def in_hbm(array):
    return pltpu.with_memory_space_constraint(array, pltpu.HBM)


def body(block_column, l_panels, u_blocks, diag_inverses, leaf_pick, merge_pick, final_order):
    rows_dev, cols = block_column.shape
    quarter = rows_dev // NX
    vmem = pl.BlockSpec(memory_space=pltpu.VMEM)
    sem = pltpu.SemaphoreType.DMA
    xs, piv = pl.pallas_call(
        kernel,
        name="panel",
        out_shape=(
            jax.ShapeDtypeStruct((256 + quarter, cols), F32),
            jax.ShapeDtypeStruct((1, cols), I32),
        ),
        in_specs=[pl.BlockSpec(memory_space=pltpu.HBM)] * 6,
        out_specs=(vmem,) * 2,
        scratch_shapes=[
            pltpu.VMEM((rows_dev * 4 + 8, 128), F32),
            pltpu.VMEM((rows_dev + 8, 128), F32),
            pltpu.VMEM((quarter, cols), F32),
            pltpu.VMEM((1, 256), I32),
            pltpu.VMEM((2, 128, 128), I32),
            pltpu.VMEM((1, 256), I32),
            pltpu.VMEM((4, 256), F32),
            pltpu.VMEM((1, 256), I32),
            pltpu.SMEM((1, 256), I32),
            pltpu.VMEM((rows_dev, 512), BF16),
            pltpu.VMEM((rows_dev, 512), BF16),
            pltpu.VMEM((NZ, NY, NC, 8, 128), F32),
            pltpu.VMEM((NY, 144, 128), F32),
            pltpu.VMEM((NY, 144, 128), F32),
            pltpu.VMEM((NY, 144, 128), F32),
            pltpu.VMEM((NY, 144, 128), F32),
            pltpu.VMEM((144, 128), F32),
            pltpu.VMEM((NZ, 9, 1, 128), F32),
            pltpu.VMEM((NZ, 9, 1, 128), F32),
            pltpu.VMEM((512, cols), BF16),
            pltpu.VMEM((512, cols), BF16),
            pltpu.VMEM((NX, 2, quarter // 2, cols), F32),
            pltpu.VMEM((6, quarter // 2, cols), F32),
            pltpu.VMEM((NX, 4, 128), F32),
            pltpu.VMEM((NZ, NY, NC, 4, 128), F32),
            pltpu.VMEM((1, 256), I32),
            pltpu.VMEM((1, 256), I32),
            pltpu.VMEM((NY, 1, 256), I32),
            pltpu.VMEM((NZ, 1, 256), I32),
            sem((9,)),
            pltpu.SemaphoreType.REGULAR,
            sem((len(SENT),)),
            sem((len(LANDED),)),
        ],
        compiler_params=pltpu.CompilerParams(
            collective_id=0, has_side_effects=True, vmem_limit_bytes=24 * 1024 * 1024
        ),
    )(
        in_hbm(l_panels.reshape(-1, 128)),
        in_hbm(block_column),
        in_hbm(u_blocks[0]),
        in_hbm(leaf_pick),
        in_hbm(merge_pick),
        in_hbm(final_order.reshape(1, -1)),
    )
    low, up, piv = pl.pallas_call(
        factor,
        name="factor",
        out_shape=(
            jax.ShapeDtypeStruct((quarter, cols), F32),
            jax.ShapeDtypeStruct((cols, cols), F32),
            jax.ShapeDtypeStruct((1, cols), I32),
        ),
        in_specs=[vmem] * 3,
        out_specs=(vmem,) * 3,
        compiler_params=pltpu.CompilerParams(vmem_limit_bytes=8 * 1024 * 1024),
    )(xs, diag_inverses, piv)
    return low, up, piv[0]


def solution(mesh):
    return jax.shard_map(
        body,
        mesh=mesh,
        in_specs=(
            P("rows", None),
            P("rows", None, "panels", None),
            P("panels", "rows", None),
            P(),
            P("rows", None),
            P(),
            P(),
        ),
        out_specs=(P(("rows", "panels"), None), P(), P()),
        check_vma=False,
    )
```

```python
import functools

import jax
import jax.numpy as jnp
from jax import lax
from jax.experimental import pallas as pl
from jax.experimental.pallas import tpu as pltpu
from jax.sharding import PartitionSpec as P

MESH = pl.DeviceIdType.MESH
F32, BF16, I32 = jnp.float32, jnp.bfloat16, jnp.int32
NZ, NY, NC, NX = 16, 4, 2, 4
FAR_FIRST = (8, 7, 9, 6, 10, 5, 11, 4, 12, 3, 13, 2, 14, 1, 15)
CLOSE = (3, 13, 2, 14, 1, 15)
NEAR = (4, 12) + CLOSE
RANGES = {"low": (0, 4), "high": (13, 16), "up": (4, 7), "down": (10, 13), "far": (7, 10),
          "w_low": (0, 6), "w_high": (11, 16), "w_far": (6, 11)}


SENT = ("uz", "ub", "uy", "uc", "pc", "py", "pz", "x", "wz", "wy", "wc", "rx", "nc", "ny", "nz")
LANDED = (
    "uz", "ub", "ub far", "uy", "uy mid", "uy far", "uc", "uc mid", "uc far", "pc0", "pc1", "pc2", "pc3", "py", "pz", "x",
    "wz low", "wz high", "wz far", "wy low", "wy high", "wc low", "wc high", "wc far", "relay1", "relay3", "rx",
    "nc", "ny", "nz",
)


def halves(v):
    hi = v.astype(BF16)
    return hi, (v - hi.astype(F32)).astype(BF16)


def mm(a, b):
    return jnp.dot(a, b, preferred_element_type=F32)


def mm3(a, b):
    ah, al = halves(a)
    bh, bl = halves(b)
    return mm(jnp.concatenate([ah, al], axis=1), jnp.concatenate([bh, bh], axis=0)) + mm(ah, bl)


def kernel(
    l_hbm, bc_hbm, u_hbm, leaf_hbm, mp_hbm, fo_hbm,
    xs, piv_ref,
    l_raw, aux_raw, own, leaf, mp, fo, u_raw, rv, rs,
    xhi, xlo, g, give, keep, rc, ry, b2, sz, rz, uhi, ulo, prod, xr, xb, w, nv, nc, ny, nz,
    in_sem, known, send_sem, recv_sem,
):
    row = lax.axis_index("rows")
    x = lax.axis_index("panels")
    z, y, c = row // (NY * NC), (row // NC) % NY, row % NC
    rows_dev = bc_hbm.shape[0]
    quarter = rows_dev // NX

    def dev(zz, yy, cc, xx):
        return ((zz * NY + yy) * NC + cc, xx)

    def zp(k):
        return (z + k) % NZ

    def yp(k):
        return (y + k) % NY

    def xp(k):
        return (x + k) % NX

    to_z = [dev(zp(k), y, c, x) for k in range(NZ)]
    to_y = [dev(z, yp(k), c, x) for k in range(NY)]
    to_x = [dev(z, y, c, xp(k)) for k in range(NX)]
    to_c = dev(z, y, 1 - c, x)

    col = pl.multiple_of((x // 2) * 128, 128)
    mine = pl.multiple_of(x * quarter, quarter)
    loads = [
        pltpu.make_async_copy(mp_hbm.at[:, pl.ds(0, 128)], mp.at[0], in_sem.at[0]),
        pltpu.make_async_copy(fo_hbm, fo, in_sem.at[1]),
        pltpu.make_async_copy(leaf_hbm, leaf, in_sem.at[2]),
        pltpu.make_async_copy(u_hbm, u_raw, in_sem.at[3]),
        pltpu.make_async_copy(mp_hbm.at[:, pl.ds(128, 128)], mp.at[1], in_sem.at[7]),
        pltpu.make_async_copy(l_hbm, l_raw.at[pl.ds(0, 4 * rows_dev), :], in_sem.at[4]),
        pltpu.make_async_copy(bc_hbm.at[:, pl.ds(col, 128)], aux_raw.at[pl.ds(0, rows_dev), :], in_sem.at[5]),
        pltpu.make_async_copy(bc_hbm.at[pl.ds(mine, quarter), :], own, in_sem.at[6]),
    ]
    barrier = pltpu.get_barrier_semaphore()
    partners = [to_z[k] for k in CLOSE] + to_y[1:] + to_x[1:] + [to_c]
    for partner in partners:
        pl.semaphore_signal(barrier, inc=1, device_id=partner, device_id_type=MESH)

    for copy in loads:
        copy.start()

    l_raw[4 * rows_dev :, :] = jnp.zeros((8, 128), F32)
    aux_raw[rows_dev:, :] = jnp.zeros((8, 128), F32)

    def copy_to(to, src, dst, out, into):
        return pltpu.make_async_remote_copy(
            src, dst, send_sem.at[SENT.index(out)], recv_sem.at[LANDED.index(into)], device_id=to, device_id_type=MESH
        )

    def send(to, src, dst, out, into):
        copy_to(to, src, dst, out, into).start()

    def arrive(into, whole):
        copy_to(to_c, whole, whole, SENT[0], into).wait_recv()

    def sent(out, whole):
        copy_to(to_c, whole, whole, out, LANDED[0]).wait_send()

    for copy in loads[3:4]:
        copy.wait()
    for i in range(4):
        for h in range(2):
            g[0, y, c, 2 * i + h : 2 * i + h + 1, :] = u_raw[i : i + 1, 128 * h : 128 * h + 128]

    for copy in loads[:3] + loads[4:5]:
        copy.wait()
    down = lax.broadcasted_iota(I32, (8, 128), 0)

    def picked(half0, half1, at):
        low = at & 127
        return jnp.where(at >= 128, jnp.take_along_axis(half1, low, axis=1), jnp.take_along_axis(half0, low, axis=1))

    def looked_up(table, first, stride, count, owner, at):
        if count < 8:
            total = jnp.zeros((8, 128), F32)
            for i in range(count):
                line = first + i * stride
                rows = [jnp.broadcast_to(table[h, line : line + 1, :], (8, 128)) for h in range(2)]
                total = jnp.where(owner == i, picked(*rows, at).astype(F32), total)
            return total
        total = jnp.zeros((8, 128), F32)
        for i in range(0, count, 8):
            rows = [table[h, pl.ds(first + i * stride, 8, stride=stride), :] for h in range(2)]
            total += jnp.where(owner - i == down, picked(*rows, at).astype(F32), 0.0)
        return jnp.broadcast_to(jnp.sum(total, axis=0, keepdims=True), (8, 128))

    for s in range(2):
        at = jnp.broadcast_to(fo[:, 128 * s : 128 * s + 128], (8, 128))
        block = jnp.zeros((8, 128), I32)
        for level in reversed(range(7)):
            found = looked_up(mp, 1 << level, 2 << level, 64 >> level, block, at).astype(I32)
            block = 2 * block + (found >> 8)
            at = found & 255
        rows = [jnp.broadcast_to(leaf[:, 128 * h : 128 * h + 128], (8, 128)) for h in range(2)]
        line = picked(*rows, at)
        rv[:, 128 * s : 128 * s + 128] = jnp.where(block == row, line, rows_dev)[0:1]
        nv[:, 128 * s : 128 * s + 128] = jnp.where(block == row, rows_dev * block + line, 0)[0:1]
    to_scalars = pltpu.make_async_copy(rv, rs, in_sem.at[8])
    to_scalars.start()

    pl.semaphore_wait(barrier, len(partners))
    for k in CLOSE:
        at = NZ - k
        send(to_z[k], g.at[0, y, c], g.at[at, y, c], "uz", "uz")

    to_scalars.wait()
    for copy in loads[5:]:
        copy.wait()

    quarter_lane = lax.broadcasted_iota(I32, (rows_dev, 128), 1) // 64 == x % 2
    wide = aux_raw[:rows_dev, :]
    aux_raw[:rows_dev, :] = jnp.where(quarter_lane, wide, pltpu.roll(wide, 64, axis=1))
    left = lax.broadcasted_iota(I32, (8, 128), 1) < 64

    def gather(into, core, k):
        base = core * 128 + yp(k) * 32
        for i in range(0, 32, 2):
            pair = rs[0, base + i], rs[0, base + i + 1]
            for n in range(8):
                into[4 * i + n : 4 * i + n + 1, :] = l_raw[pl.ds(4 * pair[n // 4] + n % 4, 1), :]
            first, second = (aux_raw[pl.ds(at, 1), :] for at in pair)
            into[128 + i // 2 : 129 + i // 2, :] = jnp.where(left[:1], first, second)

    def hand_over(k):
        gather(give.at[k], 1 - c, k)
        send(to_c, give.at[k], rc.at[k], "pc", f"pc{k}")

    def fold(k):
        gather(keep.at[k], c, k)
        arrive(f"pc{k}", rc.at[k])
        keep[k] = keep[k] + rc[k]
        send(to_y[k], keep.at[k], ry.at[k], "py", "py")

    send(to_c, nv, nc, "nc", "nc")
    hand_over(2)
    hand_over(1)
    fold(2)
    hand_over(3)
    fold(1)
    hand_over(0)
    fold(3)
    gather(keep.at[0], c, 0)
    arrive("pc0", rc.at[0])
    arrive("nc", nc)
    ny[0] = nv[...] + nc[...]
    for k in (2, 1, 3):
        send(to_y[k], ny.at[0], ny.at[k], "ny", "ny")

    def on_in_y(buf, which, out, into):
        first, last = RANGES[which]
        part = pl.ds(first, last - first)
        for k in (2, 1, 3):
            send(to_y[k], buf.at[part, y, c], buf.at[part, y, c], out, into)

    def on_to_core(buf, which, out, into):
        first, last = RANGES[which]
        part = pl.ds(first, last - first)
        send(to_c, buf.at[part, :, c], buf.at[part, :, c], out, into)

    def second(into, k, first, last, there):
        src, dst = pl.ds(first, last - first), pl.ds(there, last - first)
        send(to_z[k], g.at[src, y, c], g.at[dst, y, c], "ub", into)

    arrive("uz", g.at[pl.ds(0, 6), y, c])
    second("ub far", 11, 2, 4, 7)
    second("ub far", 5, 14, 15, 9)
    second("ub", 13, 1, 4, 4)
    second("ub", 3, 13, 16, 10)
    for k in (3, 13):
        pl.semaphore_signal(known, inc=1, device_id=to_z[k], device_id_type=MESH)

    for part in range(NX):
        rows = pl.ds(part * quarter, quarter)
        for j in range(4):
            hi, lo = halves(l_raw[pl.ds(part * quarter * 4 + j, quarter, stride=4), :])
            xhi[rows, 128 * j : 128 * j + 128] = hi
            xlo[rows, 128 * j : 128 * j + 128] = lo

    arrive("py", ry.at[pl.ds(1, 3)])
    b2[...] = keep[0] + rc[0] + ry[1] + ry[2] + ry[3]
    for zz in range(NZ):
        for line in range(9):
            at = 8 * zz + line if line < 8 else 128 + zz
            sz[zz, line] = b2[at : at + 1, :]
    pl.semaphore_wait(known, 2)
    for k in FAR_FIRST:
        send(to_z[k], sz.at[zp(k)], rz.at[k], "pz", "pz")
    on_in_y(g, "low", "uy", "uy")
    on_in_y(g, "high", "uy", "uy")
    arrive("ub", g.at[pl.ds(0, 6), y, c])
    on_in_y(g, "up", "uy", "uy mid")
    on_in_y(g, "down", "uy", "uy mid")
    arrive("ub far", g.at[pl.ds(0, 3), y, c])
    on_in_y(g, "far", "uy", "uy far")
    arrive("uy", g.at[pl.ds(0, 7), pl.ds(0, 3), c])
    on_to_core(g, "low", "uc", "uc")
    on_to_core(g, "high", "uc", "uc")
    arrive("uy mid", g.at[pl.ds(0, 6), pl.ds(0, 3), c])
    on_to_core(g, "up", "uc", "uc mid")
    on_to_core(g, "down", "uc", "uc mid")
    arrive("uy far", g.at[pl.ds(0, 3), pl.ds(0, 3), c])
    on_to_core(g, "far", "uc", "uc far")
    flat = g.reshape(NZ * NY * NC * 8, 128)

    def rounded(k):
        rows = pl.ds(pl.multiple_of(zp(k) * 32, 32), 32)
        for h in range(2):
            hi, lo = halves(flat[pl.ds(k * 64 + h, 32, stride=2), :])
            uhi[rows, 128 * h : 128 * h + 128] = hi
            ulo[rows, 128 * h : 128 * h + 128] = lo

    arrive("uc", g.at[pl.ds(0, 7), :, c])
    for k in (0, 1, 2, 3, 13, 14, 15):
        rounded(k)
    arrive("uc mid", g.at[pl.ds(0, 6), :, c])
    for k in (4, 5, 6, 10, 11, 12):
        rounded(k)
    arrive("uc far", g.at[pl.ds(0, 3), :, c])
    for k in (7, 8, 9):
        rounded(k)

    mine2 = sz[z]
    arrive("pz", rz.at[pl.ds(1, NZ - 1)])
    for k in range(1, NZ):
        mine2 = mine2 + rz[k]
    two = jnp.concatenate([jnp.concatenate([mine2[4 * i + j] for j in range(4)], axis=1) for i in range(2)], axis=0)
    two_hi = two.astype(BF16).astype(F32)
    stacked = jnp.concatenate([two_hi, two - two_hi, jnp.zeros((12, 512), F32)], axis=0).astype(BF16)
    by_hi = mm(stacked, uhi[...])
    by_lo = mm(stacked, ulo[...])
    two = by_hi[0:2] + (by_hi[2:4] + by_lo[0:2])
    both = jnp.broadcast_to(mine2[8], (8, 128))
    swapped = pltpu.roll(both, 64, axis=1)
    both = jnp.concatenate([jnp.where(left, both, swapped)[:1], jnp.where(left, swapped, both)[:1]], axis=0)
    for h in range(2):
        carried = jnp.where(quarter_lane[:2], jnp.where(x // 2 == h, both, 0.0), 0.0)
        xb[x, 2 * h : 2 * h + 2, :] = carried - two[:, 128 * h : 128 * h + 128]
    for k in (2, 1, 3):
        send(to_x[k], xb.at[x], xb.at[x], "x", "x")

    half = quarter // 2

    def partial(k):
        for h in range(2):
            rows = pl.ds(pl.multiple_of(xp(k) * quarter + h * half, half), half)
            left, right = xhi[rows, :], uhi[...]
            prod[k, h] = mm(left, right) + (mm(xlo[rows, :], right) + mm(left, ulo[...]))

    def to_neighbour(into, k, src, at):
        send(to_x[k], src, xr.at[at], "rx", into)

    partial(2)
    to_neighbour("relay1", 1, prod.at[2, 0], 0)
    to_neighbour("relay3", 3, prod.at[2, 1], 1)

    arrive("ny", ny.at[pl.ds(1, 3)])
    nz[0] = ny[0] + ny[1] + ny[2] + ny[3]
    for k in FAR_FIRST:
        send(to_z[k], nz.at[0], nz.at[k], "nz", "nz")

    arrive("x", xb.at[pl.ds(0, 3)])
    w[0, y, c] = xb[0] + xb[1] + xb[2] + xb[3]
    def far(k):
        for j in (2, 1, 3, 0):
            send(dev(zp(k), yp(j), c, x), w.at[0, y, c], w.at[NZ - k, y, c], "wz", "wz far")

    def near(k):
        send(to_z[k], w.at[0, y, c], w.at[NZ - k, y, c], "wz", "wz low" if NZ - k < 8 else "wz high")

    for step, k in ((far, 8), (far, 7), (far, 9), (near, 5), (near, 11), (far, 6), (far, 10)):
        step(k)
    for k in NEAR:
        near(k)

    partial(1)
    to_neighbour("rx", 1, prod.at[1, 1], 2)
    partial(3)
    to_neighbour("rx", 3, prod.at[3, 0], 3)
    partial(0)

    arrive("wz low", w.at[pl.ds(0, 5), y, c])
    on_in_y(w, "w_low", "wy", "wy low")
    arrive("wz high", w.at[pl.ds(0, 5), y, c])
    on_in_y(w, "w_high", "wy", "wy high")
    arrive("relay1", xr.at[0])
    prod[1, 0] = prod[1, 0] + xr[0]
    to_neighbour("rx", 1, prod.at[1, 0], 4)
    arrive("relay3", xr.at[1])
    prod[3, 1] = prod[3, 1] + xr[1]
    to_neighbour("rx", 3, prod.at[3, 1], 5)
    sent("uz", g.at[pl.ds(0, 6), y, c])
    sent("ub", g.at[pl.ds(0, 9), y, c])
    sent("uy", g.at[:, pl.ds(0, 3), c])
    sent("uc", g.at[:, :, c])
    sent("pc", give)
    sent("py", keep.at[pl.ds(0, 3)])
    sent("pz", sz.at[pl.ds(0, NZ - 1)])
    sent("x", xb.at[pl.ds(0, 3)])
    sent("nc", nv)
    sent("ny", ny.at[pl.ds(1, 3)])
    sent("nz", nz.at[pl.ds(1, NZ - 1)])
    arrive("wz far", w.at[pl.ds(0, 5), :, c])
    on_to_core(w, "w_far", "wc", "wc far")
    arrive("wy low", w.at[pl.ds(0, 6), pl.ds(0, 3), c])
    on_to_core(w, "w_low", "wc", "wc low")
    arrive("wy high", w.at[pl.ds(0, 5), pl.ds(0, 3), c])
    on_to_core(w, "w_high", "wc", "wc high")
    arrive("rx", xr.at[pl.ds(2, 4)])
    xs[2] = own[:half, :] - (prod[0, 0] + xr[3] + xr[4])
    xs[3] = own[half:, :] - (prod[0, 1] + xr[2] + xr[5])
    arrive("nz", nz.at[pl.ds(1, NZ - 1)])
    number = nz[0]
    for k in range(1, NZ):
        number = number + nz[k]
    piv_ref[...] = number

    def place(core):
        for slot in range(NY * NZ):
            for h in range(2):
                piece = w[(slot % NZ - z + NZ) % NZ, slot // NZ, core, 2 * h : 2 * h + 2, :]
                xs[core, 2 * slot : 2 * slot + 2, 128 * h : 128 * h + 128] = piece

    place(c)
    sent("wz", w.at[pl.ds(0, 15), pl.ds(0, 2), c])
    sent("wy", w.at[pl.ds(0, 11), pl.ds(0, 3), c])
    sent("rx", xr)
    arrive("wc low", w.at[pl.ds(0, 6), :, c])
    arrive("wc high", w.at[pl.ds(0, 5), :, c])
    arrive("wc far", w.at[pl.ds(0, 5), :, c])
    place(1 - c)

    sent("wc", w.at[:, :, c])


def factor(xs, dinv, piv_in, low_ref, up_ref, piv_ref):
    piv_ref[...] = piv_in[...]
    right = lax.broadcasted_iota(I32, (64, 128), 1) >= 64
    lanes = [slice(128 * h, 128 * h + 128) for h in range(2)]
    pivots = [jnp.concatenate([xs[0, :, at], xs[1, :, at]], axis=0) for at in lanes]
    rest = [jnp.concatenate([xs[2, :, at], xs[3, :, at]], axis=0) for at in lanes]
    for t in range(4):
        inverse = dinv[t]
        at, first = t // 2, 64 * (t % 2)
        u_t = [v[:64] for v in pivots]
        for h in range(2):
            if h < at:
                shown = jnp.zeros((64, 128), F32)
            else:
                shown = jnp.where(right, u_t[h], 0.0) if h == at and first else u_t[h]
            up_ref[64 * t : 64 * t + 64, 128 * h : 128 * h + 128] = shown
        panel = rest[at][:, first : first + 64]
        low_ref[:, 64 * t : 64 * t + 64] = mm3(panel, inverse)
        if t < 3:
            above = pivots[at][64:, first : first + 64]
            pivots = [v[64:] for v in pivots]
            for h in range(at + (first > 0), 2):
                step = mm3(inverse, jnp.where(right, u_t[h], 0.0) if h == at else u_t[h])
                pivots[h] = pivots[h] - mm3(above, step)
                rest[h] = rest[h] - mm3(panel, step)


def in_hbm(array):
    return pltpu.with_memory_space_constraint(array, pltpu.HBM)


def body(block_column, l_panels, u_blocks, diag_inverses, leaf_pick, merge_pick, final_order):
    rows_dev, cols = block_column.shape
    quarter = rows_dev // NX
    vmem = pl.BlockSpec(memory_space=pltpu.VMEM)
    sem = pltpu.SemaphoreType.DMA
    xs, piv = pl.pallas_call(
        kernel,
        name="panel",
        out_shape=(
            jax.ShapeDtypeStruct((4, quarter // 2, cols), F32),
            jax.ShapeDtypeStruct((1, cols), I32),
        ),
        in_specs=[pl.BlockSpec(memory_space=pltpu.HBM)] * 6,
        out_specs=(vmem,) * 2,
        scratch_shapes=[
            pltpu.VMEM((rows_dev * 4 + 8, 128), F32),
            pltpu.VMEM((rows_dev + 8, 128), F32),
            pltpu.VMEM((quarter, cols), F32),
            pltpu.VMEM((1, 256), I32),
            pltpu.VMEM((2, 128, 128), I32),
            pltpu.VMEM((1, 256), I32),
            pltpu.VMEM((4, 256), F32),
            pltpu.VMEM((1, 256), I32),
            pltpu.SMEM((1, 256), I32),
            pltpu.VMEM((rows_dev, 512), BF16),
            pltpu.VMEM((rows_dev, 512), BF16),
            pltpu.VMEM((NZ, NY, NC, 8, 128), F32),
            pltpu.VMEM((NY, 144, 128), F32),
            pltpu.VMEM((NY, 144, 128), F32),
            pltpu.VMEM((NY, 144, 128), F32),
            pltpu.VMEM((NY, 144, 128), F32),
            pltpu.VMEM((144, 128), F32),
            pltpu.VMEM((NZ, 9, 1, 128), F32),
            pltpu.VMEM((NZ, 9, 1, 128), F32),
            pltpu.VMEM((512, cols), BF16),
            pltpu.VMEM((512, cols), BF16),
            pltpu.VMEM((NX, 2, quarter // 2, cols), F32),
            pltpu.VMEM((6, quarter // 2, cols), F32),
            pltpu.VMEM((NX, 4, 128), F32),
            pltpu.VMEM((NZ, NY, NC, 4, 128), F32),
            pltpu.VMEM((1, 256), I32),
            pltpu.VMEM((1, 256), I32),
            pltpu.VMEM((NY, 1, 256), I32),
            pltpu.VMEM((NZ, 1, 256), I32),
            sem((9,)),
            pltpu.SemaphoreType.REGULAR,
            sem((len(SENT),)),
            sem((len(LANDED),)),
        ],
        compiler_params=pltpu.CompilerParams(
            collective_id=0, has_side_effects=True, vmem_limit_bytes=24 * 1024 * 1024
        ),
    )(
        in_hbm(l_panels.reshape(-1, 128)),
        in_hbm(block_column),
        in_hbm(u_blocks[0]),
        in_hbm(leaf_pick),
        in_hbm(merge_pick),
        in_hbm(final_order.reshape(1, -1)),
    )
    low, up, piv = pl.pallas_call(
        factor,
        name="factor",
        out_shape=(
            jax.ShapeDtypeStruct((quarter, cols), F32),
            jax.ShapeDtypeStruct((cols, cols), F32),
            jax.ShapeDtypeStruct((1, cols), I32),
        ),
        in_specs=[vmem] * 3,
        out_specs=(vmem,) * 3,
        compiler_params=pltpu.CompilerParams(vmem_limit_bytes=8 * 1024 * 1024),
    )(xs, diag_inverses, piv)
    return low, up, piv[0]


def solution(mesh):
    return jax.shard_map(
        body,
        mesh=mesh,
        in_specs=(
            P("rows", None),
            P("rows", None, "panels", None),
            P("panels", "rows", None),
            P(),
            P("rows", None),
            P(),
            P(),
        ),
        out_specs=(P(("rows", "panels"), None), P(), P()),
        check_vma=False,
    )
```
